1024 devices in a mesh: seq: 128 (over z, y, core), head: 8 (over x).
Axes of the slice: x: 8, y: 8, z: 8, core: 2. Of those that a mesh axis runs over, the one named last changes fastest.
Arguments:
- queries: bfloat16 [16384, 4096], P('seq', 'head'), may hold values from -6 to 6
- keys: bfloat16 [16384, 4096], P('seq', 'head'), may hold values from -0.059814453 to 0.059814453
- values: bfloat16 [16384, 4096], P('seq', 'head'), may hold values from -6 to 6
- d_out: bfloat16 [16384, 4096], P('seq', 'head'), may hold values from -6 to 6
- segment_ids: int32 [16384], P('seq'), may hold values from 0 to 7, never falling along the last dimension, each value on 1 to 4096 neighbouring positions
- decay_exps: int32 [32], P('head'), may hold values from 0 to 12
- gain: float32 [4096], P('head'), may hold values from 0.25 to 1.75
Outputs:
- normed: float32 [16384, 4096], P('seq', 'head')
- d_queries: float32 [16384, 4096], P('seq', 'head')
- d_keys: float32 [16384, 4096], P('seq', 'head')
- d_values: float32 [16384, 4096], P('seq', 'head')
The draws below stay inside these ranges and needn't reach their ends.
Inputs may be any that keep to these rules, and one draw needn't show every extreme that they name: `segment_ids`: segment ids never fall along the tokens; each document has 1 to 4096 tokens, one exactly that many.
All inputs are finite; a program needn't handle non-finite values.
Results may differ from the reference program's by a relative error of at most 0.0012.
Values sent between devices are 32-bit elements; how exact they have to be, the bound alone decides.
A program may use at most 128 MiB of HBM per device.

```python
import math
import jax
import jax.numpy as jnp
import numpy as np
from jax import lax

HEADS = 32
DH = 128
TOK_DEV = 128
DOCS = 8
TOKENS = 16384


def with_ends(values, stream_key, least, high):
    longest = values.shape.index(max(values.shape))
    spots = []
    for shift in (0, 1):
        where = [jax.random.randint(jax.random.fold_in(stream_key, axis), (), 0, length) for axis, length in enumerate(values.shape)]
        where[longest] = (where[longest] + shift) % values.shape[longest]
        spots.append(tuple(where))
    return values.at[spots[0]].set(least).at[spots[1]].set(high)


def shard_levels(own_key, dims, shards, smallest, largest):
    factor_of = 1.0
    for dim, parts in shards:
        steps = jax.random.uniform(jax.random.fold_in(jax.random.fold_in(own_key, 6), dim), (parts,), jnp.float32, smallest / len(shards), largest / len(shards))
        factor_of = factor_of * jnp.repeat(jnp.exp(steps), dims[dim] // parts).reshape((-1,) + (1,) * (len(dims) - 1 - dim))
    return factor_of


def profile(number_of, total, bound, slope):
    loads = [(1 << 20) // math.isqrt(rank ** slope) + 1 for rank in range(2, number_of + 1)]
    rest, given = total - bound - (number_of - 1), [1] * (number_of - 1)
    while rest > 0:
        free = [i for i in range(number_of - 1) if given[i] < bound]
        pool, budget = sum([loads[i] for i in free]), rest
        for i in free:
            more = min(bound - given[i], max(1, budget * loads[i] // pool), rest)
            given[i] = given[i] + more
            rest = rest - more
    return np.array([bound] + given)


def ragged_sizes(key, count, total, reach, skew):
    if count == 2:
        one = jax.random.randint(key, (), max(1, total - reach), min(reach, total - 1) + 1)
        return jnp.stack([one, total - one])
    tallies = jnp.asarray(profile(count, total, reach, skew), jnp.int32)
    twos = (count - 1) // 2
    donor, receiver = tallies[1:1 + 2 * twos:2], tallies[2:2 + 2 * twos:2]
    margin = jnp.minimum(donor - 1, reach - receiver)
    moved = jax.random.randint(jax.random.fold_in(key, 1), (twos,), 0, 1 << 20) % (margin + 1)
    tallies = tallies.at[1:1 + 2 * twos:2].set(donor - moved).at[2:2 + 2 * twos:2].set(receiver + moved)
    return tallies[jax.random.permutation(jax.random.fold_in(key, 2), count)]


def noise(own_key, shape, deviation, bound, shards=(), kind=jnp.bfloat16):
    values = deviation * jax.random.normal(own_key, shape, jnp.float32)
    if shards:
        values = values * shard_levels(own_key, shape, shards, -0.22, 0.18)
    return jnp.clip(values, -bound, bound).astype(kind)


def setup_inputs(seed: int = 0) -> dict:
    seeds = jax.random.split(jax.random.key(seed), 8)
    queries = noise(seeds[0], (TOKENS, HEADS * DH), 1.0, 6.0, ((0, 128), (1, 8)))
    keys = noise(seeds[1], (TOKENS, HEADS * DH), 0.01, 0.059814453, ((0, 128), (1, 8)))
    values = noise(seeds[2], (TOKENS, HEADS * DH), 1.0, 6.0, ((0, 128), (1, 8)))
    d_out = noise(seeds[3], (TOKENS, HEADS * DH), 1.0, 6.0, ((0, 128), (1, 8)))
    segment_ids = jnp.searchsorted(jnp.cumsum(ragged_sizes(seeds[4], DOCS, TOKENS, TOKENS // 4, 2)), jnp.arange(TOKENS), side="right").astype(jnp.int32)
    decay_exps = with_ends(jax.random.randint(seeds[5], (HEADS,), 0, 13), jax.random.fold_in(seeds[5], 1), 0, 12).astype(jnp.int32)
    gain = jnp.clip(1.0 + 0.15 * jax.random.normal(seeds[6], (HEADS * DH,), jnp.float32), 0.25, 1.75)
    return dict(queries=queries, keys=keys, values=values, d_out=d_out, segment_ids=segment_ids, decay_exps=decay_exps, gain=gain)


EPSILON = 1e-06
HIGH = lax.Precision.HIGHEST

def tables(seg_block, decay_rate, block_len):
    place = jnp.arange(block_len, dtype=jnp.float32)
    distance = place[:, None] - place[None, :]
    causal_mask = (distance >= 0) & (seg_block[:, None] == seg_block[None, :])
    decay = jnp.where(causal_mask[None], jnp.exp(-decay_rate[:, None, None] * jnp.maximum(distance, 0.0)[None]), 0.0)
    return (place, decay)

def block_scores(queries_h, keys_h, values_h, grads_h, decay):
    scores = (jnp.einsum('thd,shd->hts', queries_h, keys_h, precision=HIGH) * decay).astype(jnp.bfloat16)
    grad_scores = (jnp.einsum('the,she->hts', grads_h, values_h, precision=HIGH) * decay).astype(jnp.bfloat16)
    return (scores.astype(jnp.float32), grad_scores.astype(jnp.float32))

def reference(queries, keys, values, d_out, segment_ids, decay_exps, gain):
    head_count = HEADS
    block_len = TOK_DEV
    blocks = TOKENS // block_len
    decay_rate = jnp.exp2(decay_exps.astype(jnp.float32)) / TOKENS
    span_decay = jnp.exp(-decay_rate * block_len)

    def shaped(array):
        return array.reshape(blocks, block_len, head_count, DH)
    stacked = (shaped(queries), shaped(keys), shaped(values), shaped(d_out), segment_ids.reshape(blocks, block_len))

    def widen(inputs):
        return tuple((item.astype(jnp.float32) for item in inputs[:4])) + (inputs[4],)

    def forward_step(carry, inputs):
        state, last_seg = carry
        queries_h, keys_h, values_h, grads_h, seg_block = widen(inputs)
        place, decay = tables(seg_block, decay_rate, block_len)
        scores, grad_scores = block_scores(queries_h, keys_h, values_h, grads_h, decay)
        inflow = jnp.exp(-decay_rate[None, :] * (place + 1.0)[:, None]) * (seg_block == last_seg)[:, None]
        output = jnp.einsum('hts,she->the', scores, values_h, precision=HIGH)
        output = output + inflow[:, :, None] * jnp.einsum('thd,hde->the', queries_h, state, precision=HIGH)
        grad_q = jnp.einsum('hts,shd->thd', grad_scores, keys_h, precision=HIGH)
        grad_q = grad_q + inflow[:, :, None] * jnp.einsum('the,hde->thd', grads_h, state, precision=HIGH)
        endw = jnp.exp(-decay_rate[None, :] * (block_len - 1.0 - place)[:, None]) * (seg_block == seg_block[-1])[:, None]
        local_state = jnp.einsum('th,thd,the->hde', endw, keys_h, values_h, precision=HIGH)
        keep_on = (seg_block[-1] == last_seg).astype(jnp.float32)
        state = keep_on * span_decay[:, None, None] * state + local_state
        return ((state, seg_block[-1]), (output, grad_q))
    start_state = jnp.zeros((head_count, DH, DH), jnp.float32)
    _, (output, grad_q) = lax.scan(forward_step, (start_state, jnp.int32(-1)), stacked)

    def backward_step(carry, inputs):
        grad_state, next_first = carry
        queries_h, keys_h, values_h, grads_h, seg_block = widen(inputs)
        place, decay = tables(seg_block, decay_rate, block_len)
        scores, grad_scores = block_scores(queries_h, keys_h, values_h, grads_h, decay)
        outw = jnp.exp(-decay_rate[None, :] * (block_len - place)[:, None]) * (seg_block == next_first)[:, None]
        grad_k = jnp.einsum('hts,thd->shd', grad_scores, queries_h, precision=HIGH)
        grad_k = grad_k + outw[:, :, None] * jnp.einsum('she,hde->shd', values_h, grad_state, precision=HIGH)
        grad_v = jnp.einsum('hts,the->she', scores, grads_h, precision=HIGH)
        grad_v = grad_v + outw[:, :, None] * jnp.einsum('shd,hde->she', keys_h, grad_state, precision=HIGH)
        startw = jnp.exp(-decay_rate[None, :] * place[:, None]) * (seg_block == seg_block[0])[:, None]
        local_state = jnp.einsum('th,thd,the->hde', startw, queries_h, grads_h, precision=HIGH)
        keep_on = (seg_block[0] == next_first).astype(jnp.float32)
        grad_state = keep_on * span_decay[:, None, None] * grad_state + local_state
        return ((grad_state, seg_block[0]), (grad_k, grad_v))
    _, (grad_k, grad_v) = lax.scan(backward_step, (start_state, jnp.int32(-1)), stacked, reverse=True)
    output = output.reshape(TOKENS, head_count, DH)
    mean_sq = lax.optimization_barrier(jnp.mean(output * output, axis=(1, 2)))
    normed = output * lax.rsqrt(mean_sq + EPSILON)[:, None, None] * gain.reshape(head_count, DH)[None]
    width = head_count * DH
    return (normed.reshape(TOKENS, width), grad_q.reshape(TOKENS, width), grad_k.reshape(TOKENS, width), grad_v.reshape(TOKENS, width))
```

```python
import functools

import jax
import jax.numpy as jnp
from jax import lax
from jax.experimental import pallas as pl
from jax.experimental.pallas import tpu as pltpu
from jax.sharding import PartitionSpec as P

DH = 128
BLK = 128
NH = 4
OWN = 2
ROW = 8
EPSILON = 1e-06
MESH = pl.DeviceIdType.MESH
F32 = jnp.float32
BF16 = jnp.bfloat16

NN = (((1,), (0,)), ((), ()))
NT = (((1,), (1,)), ((), ()))
TN = (((0,), (0,)), ((), ()))


def dot(a, b, dims):
    return lax.dot_general(a, b, dims, preferred_element_type=F32)


def split(a):
    high = a.astype(BF16)
    return high, (a - high.astype(F32)).astype(BF16)


def kernel(
    zs, xs, exps, seg, q, k, v, g, gain,
    normed, dq, dk, dv,
    local, part, mymeta, pmeta, chip, cmeta, rmeta, there, zsend, zrecv, slices, raw, give, state, out, xsend, xrecv,
    d_send, d_recv, m_send, m_recv, t_send, t_recv, z_send, z_recv, b_send, b_recv, e_send, e_recv, x_send, x_recv,
):
    s, x = lax.axis_index("seq"), lax.axis_index("head")
    c, y, z = s % 2, (s // 2) % ROW, s // (2 * ROW)
    width = BLK // ROW
    total_tokens = BLK * 2 * ROW * zs

    def at(zz, yy, cc):
        return ((zz * ROW + yy) * 2 + cc, x)

    partner = at(z, y, 1 - c)
    in_row = [(y + n) % ROW for n in range(1, ROW)]

    def hop(way, n):
        return at((z + (n if way == 0 else zs - n)) % zs, y, c)

    def copy(src, dst, send, recv, device):
        return pltpu.make_async_remote_copy(
            src_ref=src, dst_ref=dst, send_sem=send, recv_sem=recv, device_id=device, device_id_type=MESH
        )

    barrier = pltpu.get_barrier_semaphore()
    others = [partner] + [at(z, j, c) for j in in_row] + [hop(w, n) for w in (0, 1) for n in (1, 2)]
    others += [(s, (x + n) % xs) for n in range(1, xs)]
    for device in others:
        pl.semaphore_signal(barrier, inc=1, device_id=device, device_id_type=MESH)

    place = lax.broadcasted_iota(jnp.int32, (BLK, DH), 0).astype(F32)
    seg_row = seg[...].astype(F32)
    seg_rows = jnp.broadcast_to(seg_row, (BLK, BLK))
    seg_cols = seg_rows.T
    first = jnp.broadcast_to(seg_cols[0:1, :], (8, DH))
    last = jnp.broadcast_to(seg_cols[BLK - 1 : BLK, :], (8, DH))
    row_id = lax.broadcasted_iota(jnp.int32, (8, DH), 0)
    mymeta[...] = jnp.where(row_id == 0, first, last)

    def rate_of(h):
        whole = jnp.left_shift(jnp.ones((1, DH), jnp.int32), jnp.full((1, DH), exps[h], jnp.int32))
        return whole.astype(F32) / total_tokens

    rates = [rate_of(h) for h in range(NH)]
    own_rates = [rate_of(OWN * c + i) for i in range(OWN)]
    cols = [slice(h * DH, (h + 1) * DH) for h in range(NH)]

    def weighted(weight, left, right):
        high, low = split(weight * left.astype(F32))
        return dot(high, right, TN) + dot(low, right, TN)

    ends = (seg_cols == last[0:1, :]).astype(F32)
    starts = (seg_cols == first[0:1, :]).astype(F32)
    for h in range(NH):
        weight = jnp.exp(-rates[h] * (BLK - 1.0 - place)) * ends
        local[0, h] = weighted(weight, k[:, cols[h]], v[:, cols[h]])

    pl.semaphore_wait(barrier, len(others))

    meta_copy = copy(mymeta, pmeta, m_send.at[0], m_recv.at[0], partner)
    meta_copy.start()
    sends = [meta_copy]

    def to_partner(way):
        found = []
        for i in range(OWN):
            found.append(
                copy(local.at[way, OWN * (1 - c) + i], part.at[way, i], d_send.at[way, i], d_recv.at[way, i], partner)
            )
            found[-1].start()
        sends.extend(found)
        return found

    first_copies = [to_partner(0)]
    for h in range(NH):
        weight = jnp.exp(-rates[h] * place) * starts
        local[1, h] = weighted(weight, q[:, cols[h]], g[:, cols[h]])
    first_copies.append(to_partner(1))

    meta_copy.wait_recv()
    firsts = [jnp.where(c == 0, mymeta[0:1, :], pmeta[0:1, :]), jnp.where(c == 0, pmeta[0:1, :], mymeta[0:1, :])]
    lasts = [jnp.where(c == 0, mymeta[1:2, :], pmeta[1:2, :]), jnp.where(c == 0, pmeta[1:2, :], mymeta[1:2, :])]
    chip_meta = jnp.where(row_id == 0, jnp.broadcast_to(firsts[0], (8, DH)), jnp.broadcast_to(lasts[1], (8, DH)))
    cmeta[...] = chip_meta
    rmeta[y] = chip_meta
    row_meta = []
    for n, j in enumerate(in_row):
        row_meta.append(copy(cmeta, rmeta.at[y], m_send.at[1 + n], m_recv.at[1 + y], at(z, j, c)))
        row_meta[-1].start()
    sends.extend(row_meta)
    same_chip = [(lasts[0] == lasts[1]).astype(F32), (firsts[0] == firsts[1]).astype(F32)]

    def to_row(way):
        for i in range(OWN):
            first_copies[way][i].wait_recv()
            carried = jnp.exp(-own_rates[i] * BLK) * same_chip[way]
            mine = jnp.where(c == 1 - way, 1.0, carried)
            theirs = jnp.where(c == 1 - way, carried, 1.0)
            whole = mine * local[way, OWN * c + i] + theirs * part[way, i]
            chip[way, i] = whole
            there[way, i, y] = chip[way, i, pl.ds(pl.multiple_of(y * width, width), width), :]
            for n, j in enumerate(in_row):
                sends.append(
                    copy(
                        chip.at[way, i, pl.ds(pl.multiple_of(j * width, width), width)],
                        there.at[way, i, y],
                        t_send.at[way, i, n],
                        t_recv.at[way, i, y],
                        at(z, j, c),
                    )
                )
                sends[-1].start()

    to_row(0)
    to_row(1)

    distance = place - lax.broadcasted_iota(jnp.int32, (BLK, DH), 1).astype(F32)
    causal = (distance >= 0) & (seg_cols == seg_rows)
    reach = jnp.maximum(distance, 0.0)

    def within(h):
        decay = jnp.where(causal, jnp.exp(-rates[h] * reach), 0.0)
        qh, kh, vh, gh = q[:, cols[h]], k[:, cols[h]], v[:, cols[h]], g[:, cols[h]]
        scores = (dot(qh, kh, NT) * decay).astype(BF16)
        grad_scores = (dot(gh, vh, NT) * decay).astype(BF16)
        out[:, cols[h]] = dot(scores, vh, NN)
        dq[:, cols[h]] = dot(grad_scores, kh, NN)
        dk[:, cols[h]] = dot(grad_scores, qh, TN)
        dv[:, cols[h]] = dot(scores, gh, TN)

    within(0)
    within(1)

    for j in in_row:
        copy(cmeta, rmeta.at[j], m_send.at[0], m_recv.at[1 + j], partner).wait_recv()

    def end_of(way, j):
        return rmeta[j, 1:2, :] if way == 0 else rmeta[j, 0:1, :]

    orders = [list(range(ROW)), list(range(ROW))[::-1]]

    def to_rows(way):
        order = orders[way]
        zsend[way, 0:8] = jnp.broadcast_to(end_of(way, order[-1]), (8, DH))
        for i in range(OWN):
            for j in in_row:
                copy(
                    there.at[way, i, y], there.at[way, i, j], t_send.at[way, i, 0], t_recv.at[way, i, j], partner
                ).wait_recv()
            span = jnp.exp(-own_rates[i] * (2 * BLK))
            sofar = there[way, i, order[0]]
            for n in range(1, ROW):
                slices[way, i, order[n]] = sofar
                keep = span * (end_of(way, order[n]) == end_of(way, order[n - 1])).astype(F32)
                sofar = there[way, i, order[n]] + keep * sofar
            low, high = (0, 8 + width) if i == 0 else (8 + width, 8 + 2 * width)
            zsend[way, 8 + i * width : 8 + (i + 1) * width] = sofar
            for n in (1, 2):
                sends.append(
                    copy(
                        zsend.at[way, low:high],
                        zrecv.at[way, n - 1, low:high],
                        z_send.at[way, n - 1, i],
                        z_recv.at[way, n - 1, i],
                        hop(way, n),
                    )
                )
                sends[-1].start()

    to_rows(0)
    to_rows(1)
    within(2)
    within(3)

    edge = [None, None]

    def to_chips(way):
        order = orders[way]
        left = z if way == 0 else zs - 1 - z
        for i in range(OWN):
            low, high = (0, 8 + width) if i == 0 else (8 + width, 8 + 2 * width)
            for n in (1, 2):
                copy(
                    zsend.at[way, low:high],
                    zrecv.at[way, n - 1, low:high],
                    z_send.at[way, n - 1, i],
                    z_recv.at[way, n - 1, i],
                    partner,
                ).wait_recv()
            if i == 0:
                near = jnp.where(left >= 1, zrecv[way, 0, 0:1], -1.0)
                far = jnp.where(left >= 2, zrecv[way, 1, 0:1], -2.0)
                edge[way] = near
            span = jnp.exp(-own_rates[i] * (2 * BLK))
            row_span = jnp.exp(-own_rates[i] * (2 * BLK * ROW)) * (near == far).astype(F32)
            rows = slice(8 + i * width, 8 + (i + 1) * width)
            entering = jnp.where(left >= 1, zrecv[way, 0, rows] + row_span * zrecv[way, 1, rows], 0.0)
            keep = jnp.ones((1, DH), F32)
            before = near
            for n in range(ROW):
                j = order[n]
                if n == 0:
                    slices[way, i, j] = entering
                else:
                    slices[way, i, j] = slices[way, i, j] + keep * entering
                here = end_of(way, j)
                keep = keep * span * (here == before).astype(F32)
                before = here
            mine = pl.ds(pl.multiple_of(y * width, width), width)
            raw[way, i, mine] = slices[way, i, y]
            for n, j in enumerate(in_row):
                sends.append(
                    copy(
                        slices.at[way, i, j],
                        raw.at[way, i, mine],
                        b_send.at[way, i, n],
                        b_recv.at[way, i, y],
                        at(z, j, c),
                    )
                )
                sends[-1].start()

    to_chips(0)
    to_chips(1)

    beside = []
    for way in (0, 1):
        neighbour = rmeta[(y + ROW - 1) % ROW, 1:2, :] if way == 0 else rmeta[(y + 1) % ROW, 0:1, :]
        beside.append(jnp.where(y == (0 if way == 0 else ROW - 1), edge[way], neighbour))

    def to_core(way):
        inner = lasts[0] if way == 0 else firsts[1]
        kept = (inner == beside[way]).astype(F32)
        for i in range(OWN):
            for j in in_row:
                theirs = pl.ds(pl.multiple_of(j * width, width), width)
                copy(
                    slices.at[way, i, j], raw.at[way, i, theirs], b_send.at[way, i, 0], b_recv.at[way, i, j], partner
                ).wait_recv()
            outer = raw[way, i]
            between = jnp.where(c == way, local[way, OWN * c + i], part[way, i])
            inside = between + jnp.exp(-own_rates[i] * BLK) * kept * outer
            state[way, OWN * c + i] = jnp.where(c == way, outer, inside)
            give[way, i] = jnp.where(c == way, inside, outer)
            sends.append(
                copy(
                    give.at[way, i],
                    state.at[way, OWN * c + i],
                    e_send.at[way, i],
                    e_recv.at[way, i],
                    partner,
                )
            )
            sends[-1].start()

    def from_core(way):
        for i in range(OWN):
            copy(
                give.at[way, i], state.at[way, OWN * (1 - c) + i], e_send.at[way, i], e_recv.at[way, i], partner
            ).wait_recv()

    to_core(0)
    from_core(0)

    seg_before = jnp.where(c == 0, beside[0], lasts[0])
    seg_after = jnp.where(c == 1, beside[1], firsts[1])
    joins = (seg_cols == seg_before).astype(F32)
    leaves = (seg_cols == seg_after).astype(F32)

    squares = None
    for h in range(NH):
        inflow = jnp.exp(-rates[h] * (place + 1.0)) * joins
        high, low = split(state[0, h])
        qh = q[:, cols[h]]
        whole = out[:, cols[h]] + inflow * (dot(qh, high, NN) + dot(qh, low, NN))
        out[:, cols[h]] = whole
        squares = whole * whole if h == 0 else squares + whole * whole
    mine = jnp.broadcast_to(jnp.sum(squares.T, axis=0, keepdims=True), (8, DH))
    xsend[...] = mine
    xrecv[x] = mine
    for n in range(1, xs):
        sends.append(copy(xsend, xrecv.at[x], x_send.at[n - 1], x_recv.at[x], (s, (x + n) % xs)))
        sends[-1].start()

    to_core(1)
    for h in range(NH):
        inflow = jnp.exp(-rates[h] * (place + 1.0)) * joins
        high, low = split(state[0, h])
        gh = g[:, cols[h]]
        dq[:, cols[h]] = dq[:, cols[h]] + inflow * (dot(gh, high, NT) + dot(gh, low, NT))
    from_core(1)
    for h in range(NH):
        outflow = jnp.exp(-rates[h] * (BLK - place)) * leaves
        high, low = split(state[1, h])
        kh, vh = k[:, cols[h]], v[:, cols[h]]
        dk[:, cols[h]] = dk[:, cols[h]] + outflow * (dot(vh, high, NT) + dot(vh, low, NT))
        dv[:, cols[h]] = dv[:, cols[h]] + outflow * (dot(kh, high, NN) + dot(kh, low, NN))

    for n in range(1, xs):
        from_x = (x + n) % xs
        copy(xsend, xrecv.at[from_x], x_send.at[n - 1], x_recv.at[from_x], partner).wait_recv()
    summed = xrecv[0]
    for n in range(1, xs):
        summed = summed + xrecv[n]
    inverse = lax.rsqrt(summed / (NH * DH * xs) + EPSILON)
    scale = jnp.broadcast_to(inverse[0:1, :], (BLK, BLK)).T
    for h in range(NH):
        normed[:, cols[h]] = out[:, cols[h]] * scale * gain[:, cols[h]]

    for sent in sends:
        sent.wait_send()


def body(zs, xs, queries, keys, values, d_out, segment_ids, decay_exps, gain):
    width = BLK // ROW
    vmem = pl.BlockSpec(memory_space=pltpu.VMEM)
    dma = pltpu.SemaphoreType.DMA
    result = jax.ShapeDtypeStruct((BLK, NH * DH), F32)
    return pl.pallas_call(
        functools.partial(kernel, zs, xs),
        out_shape=(result,) * 4,
        in_specs=[pl.BlockSpec(memory_space=pltpu.SMEM)] + [vmem] * 6,
        out_specs=(vmem,) * 4,
        scratch_shapes=[
            pltpu.VMEM((2, NH, DH, DH), F32),
            pltpu.VMEM((2, OWN, DH, DH), F32),
            pltpu.VMEM((8, DH), F32),
            pltpu.VMEM((8, DH), F32),
            pltpu.VMEM((2, OWN, DH, DH), F32),
            pltpu.VMEM((8, DH), F32),
            pltpu.VMEM((ROW, 8, DH), F32),
            pltpu.VMEM((2, OWN, ROW, width, DH), F32),
            pltpu.VMEM((2, 8 + OWN * width, DH), F32),
            pltpu.VMEM((2, 2, 8 + OWN * width, DH), F32),
            pltpu.VMEM((2, OWN, ROW, width, DH), F32),
            pltpu.VMEM((2, OWN, DH, DH), F32),
            pltpu.VMEM((2, OWN, DH, DH), F32),
            pltpu.VMEM((2, NH, DH, DH), F32),
            pltpu.VMEM((BLK, NH * DH), F32),
            pltpu.VMEM((8, DH), F32),
            pltpu.VMEM((xs, 8, DH), F32),
            dma((2, OWN)), dma((2, OWN)),
            dma((1 + ROW,)), dma((1 + ROW,)),
            dma((2, OWN, ROW)), dma((2, OWN, ROW)),
            dma((2, 2, OWN)), dma((2, 2, OWN)),
            dma((2, OWN, ROW)), dma((2, OWN, ROW)),
            dma((2, OWN)), dma((2, OWN)),
            dma((xs,)), dma((xs,)),
        ],
        compiler_params=pltpu.CompilerParams(
            collective_id=0, has_side_effects=True, vmem_limit_bytes=32 << 20
        ),
        name="attention",
    )(decay_exps, segment_ids.reshape(1, BLK), queries, keys, values, d_out, gain.reshape(1, NH * DH))


def solution(mesh):
    both = P("seq", "head")
    return jax.shard_map(
        functools.partial(body, mesh.shape["seq"] // (2 * ROW), mesh.shape["head"]),
        mesh=mesh,
        in_specs=(both, both, both, both, P("seq"), P("head"), P("head")),
        out_specs=(both, both, both, both),
        check_vma=False,
    )
```

```python
import functools

import jax
import jax.numpy as jnp
from jax import lax
from jax.experimental import pallas as pl
from jax.experimental.pallas import tpu as pltpu
from jax.sharding import PartitionSpec as P

DH = 128
BLK = 128
NH = 4
OWN = 2
ROW = 8
EPSILON = 1e-06
MESH = pl.DeviceIdType.MESH
F32 = jnp.float32
BF16 = jnp.bfloat16

NN = (((1,), (0,)), ((), ()))
NT = (((1,), (1,)), ((), ()))
TN = (((0,), (0,)), ((), ()))


def dot(a, b, dims):
    return lax.dot_general(a, b, dims, preferred_element_type=F32)


def split(a):
    high = a.astype(BF16)
    return high, (a - high.astype(F32)).astype(BF16)


def kernel(
    zs, xs, exps_in, seg_in, q_in, k_in, v_in, g_in, gain_in,
    normed, dq, dk, dv,
    exps, seg, q, k, v, g, gain,
    local, part, mymeta, pmeta, chip, cmeta, rmeta, there, zsend, zrecv, slices, raw, give, state, out, xsend, xrecv,
    loads, d_send, d_recv, m_send, m_recv, t_send, t_recv, z_send, z_recv, b_send, b_recv, e_send, e_recv, x_send, x_recv,
):
    s, x = lax.axis_index("seq"), lax.axis_index("head")
    c, y, z = s % 2, (s // 2) % ROW, s // (2 * ROW)
    width = BLK // ROW
    total_tokens = BLK * 2 * ROW * zs

    def at(zz, yy, cc):
        return ((zz * ROW + yy) * 2 + cc, x)

    partner = at(z, y, 1 - c)
    in_row = [(y + n) % ROW for n in range(1, ROW)]

    def hop(way, n):
        return at((z + (n if way == 0 else zs - n)) % zs, y, c)

    def copy(src, dst, send, recv, device):
        return pltpu.make_async_remote_copy(
            src_ref=src, dst_ref=dst, send_sem=send, recv_sem=recv, device_id=device, device_id_type=MESH
        )

    def after(way):
        return zs - 1 - z if way == 0 else z

    def before(way):
        return after(1 - way)

    barrier = pltpu.get_barrier_semaphore()
    others = [partner] + [at(z, j, c) for j in in_row] + [(s, (x + n) % xs) for n in range(1, xs)]
    for device in others:
        pl.semaphore_signal(barrier, inc=1, device_id=device, device_id_type=MESH)
    hops = [(w, n) for w in (0, 1) for n in (1, 2)]
    for w, n in hops:

        @pl.when(after(w) >= n)
        def _():
            pl.semaphore_signal(barrier, inc=1, device_id=hop(w, n), device_id_type=MESH)

    fetches = [
        pltpu.make_async_copy(src, dst, loads.at[n])
        for n, (src, dst) in enumerate(
            [(seg_in, seg), (exps_in, exps), (k_in, k), (v_in, v), (q_in, q), (g_in, g), (gain_in, gain)]
        )
    ]
    for fetch in fetches:
        fetch.start()
    for w, n in hops:

        @pl.when(before(w) < n)
        def _():
            zrecv[w, n - 1, 0:8] = jnp.full((8, DH), -float(n), F32)
            zrecv[w, n - 1, 8:] = jnp.zeros((OWN * width, DH), F32)

    for fetch in fetches[:4]:
        fetch.wait()

    place = lax.broadcasted_iota(jnp.int32, (BLK, DH), 0).astype(F32)
    seg_row = seg[...].astype(F32)
    seg_rows = jnp.broadcast_to(seg_row, (BLK, BLK))
    seg_cols = seg_rows.T
    first = jnp.broadcast_to(seg_cols[0:1, :], (8, DH))
    last = jnp.broadcast_to(seg_cols[BLK - 1 : BLK, :], (8, DH))
    row_id = lax.broadcasted_iota(jnp.int32, (8, DH), 0)
    mymeta[...] = jnp.where(row_id == 0, first, last)

    def rate_of(h):
        whole = jnp.left_shift(jnp.ones((1, DH), jnp.int32), jnp.full((1, DH), exps[h], jnp.int32))
        return whole.astype(F32) / total_tokens

    rates = [rate_of(h) for h in range(NH)]
    own_rates = [rate_of(OWN * c + i) for i in range(OWN)]
    cols = [slice(h * DH, (h + 1) * DH) for h in range(NH)]

    def weighted(weight, left, right):
        high, low = split(weight * left.astype(F32))
        return dot(high, right, TN) + dot(low, right, TN)

    ends = (seg_cols == last[0:1, :]).astype(F32)
    starts = (seg_cols == first[0:1, :]).astype(F32)
    for h in range(NH):
        weight = jnp.exp(-rates[h] * (BLK - 1.0 - place)) * ends
        local[0, h] = weighted(weight, k[:, cols[h]], v[:, cols[h]])

    pl.semaphore_wait(barrier, len(others) + jnp.minimum(z, 2) + jnp.minimum(zs - 1 - z, 2))

    meta_copy = copy(mymeta, pmeta, m_send.at[0], m_recv.at[0], partner)
    meta_copy.start()
    sends = [meta_copy]

    def to_partner(way):
        found = []
        for i in range(OWN):
            found.append(
                copy(local.at[way, OWN * (1 - c) + i], part.at[way, i], d_send.at[way, i], d_recv.at[way, i], partner)
            )
            found[-1].start()
        sends.extend(found)
        return found

    first_copies = [to_partner(0)]
    for fetch in fetches[4:]:
        fetch.wait()
    for h in range(NH):
        weight = jnp.exp(-rates[h] * place) * starts
        local[1, h] = weighted(weight, q[:, cols[h]], g[:, cols[h]])
    first_copies.append(to_partner(1))

    meta_copy.wait_recv()
    firsts = [jnp.where(c == 0, mymeta[0:1, :], pmeta[0:1, :]), jnp.where(c == 0, pmeta[0:1, :], mymeta[0:1, :])]
    lasts = [jnp.where(c == 0, mymeta[1:2, :], pmeta[1:2, :]), jnp.where(c == 0, pmeta[1:2, :], mymeta[1:2, :])]
    chip_meta = jnp.where(row_id == 0, jnp.broadcast_to(firsts[0], (8, DH)), jnp.broadcast_to(lasts[1], (8, DH)))
    cmeta[...] = chip_meta
    rmeta[y] = chip_meta
    row_meta = []
    for n, j in enumerate(in_row):
        row_meta.append(copy(cmeta, rmeta.at[y], m_send.at[1 + n], m_recv.at[1 + y], at(z, j, c)))
        row_meta[-1].start()
    sends.extend(row_meta)
    same_chip = [(lasts[0] == lasts[1]).astype(F32), (firsts[0] == firsts[1]).astype(F32)]

    def to_row(way):
        for i in range(OWN):
            first_copies[way][i].wait_recv()
            carried = jnp.exp(-own_rates[i] * BLK) * same_chip[way]
            mine = jnp.where(c == 1 - way, 1.0, carried)
            theirs = jnp.where(c == 1 - way, carried, 1.0)
            whole = mine * local[way, OWN * c + i] + theirs * part[way, i]
            chip[way, i] = whole
            there[way, i, y] = chip[way, i, pl.ds(pl.multiple_of(y * width, width), width), :]
            for n, j in enumerate(in_row):
                sends.append(
                    copy(
                        chip.at[way, i, pl.ds(pl.multiple_of(j * width, width), width)],
                        there.at[way, i, y],
                        t_send.at[way, i, n],
                        t_recv.at[way, i, y],
                        at(z, j, c),
                    )
                )
                sends[-1].start()

    to_row(0)
    to_row(1)

    distance = place - lax.broadcasted_iota(jnp.int32, (BLK, DH), 1).astype(F32)
    causal = (distance >= 0) & (seg_cols == seg_rows)
    reach = jnp.maximum(distance, 0.0)

    def within(h):
        decay = jnp.where(causal, jnp.exp(-rates[h] * reach), 0.0)
        qh, kh, vh, gh = q[:, cols[h]], k[:, cols[h]], v[:, cols[h]], g[:, cols[h]]
        scores = (dot(qh, kh, NT) * decay).astype(BF16)
        grad_scores = (dot(gh, vh, NT) * decay).astype(BF16)
        out[:, cols[h]] = dot(scores, vh, NN)
        dq[:, cols[h]] = dot(grad_scores, kh, NN)
        dk[:, cols[h]] = dot(grad_scores, qh, TN)
        dv[:, cols[h]] = dot(scores, gh, TN)

    within(0)
    within(1)

    for j in in_row:
        copy(cmeta, rmeta.at[j], m_send.at[0], m_recv.at[1 + j], partner).wait_recv()

    def end_of(way, j):
        return rmeta[j, 1:2, :] if way == 0 else rmeta[j, 0:1, :]

    def z_copy(way, n, i):
        rows = slice(0, 8 + width) if i == 0 else slice(8 + width, 8 + 2 * width)
        return copy(
            zsend.at[way, rows], zrecv.at[way, n - 1, rows], z_send.at[way, n - 1, i], z_recv.at[way, n - 1, i], hop(way, n)
        )

    orders = [list(range(ROW)), list(range(ROW))[::-1]]

    def to_rows(way):
        order = orders[way]
        zsend[way, 0:8] = jnp.broadcast_to(end_of(way, order[-1]), (8, DH))
        for i in range(OWN):
            for j in in_row:
                copy(
                    there.at[way, i, y], there.at[way, i, j], t_send.at[way, i, 0], t_recv.at[way, i, j], partner
                ).wait_recv()
            span = jnp.exp(-own_rates[i] * (2 * BLK))
            sofar = there[way, i, order[0]]
            for n in range(1, ROW):
                slices[way, i, order[n]] = sofar
                keep = span * (end_of(way, order[n]) == end_of(way, order[n - 1])).astype(F32)
                sofar = there[way, i, order[n]] + keep * sofar
            zsend[way, 8 + i * width : 8 + (i + 1) * width] = sofar
            for n in (1, 2):
                @pl.when(after(way) >= n)
                def _():
                    z_copy(way, n, i).start()

    to_rows(0)
    to_rows(1)
    within(2)
    within(3)

    edge = [None, None]

    def to_chips(way):
        order = orders[way]
        for i in range(OWN):
            for n in (1, 2):

                @pl.when(before(way) >= n)
                def _():
                    z_copy(way, n, i).wait_recv()

            if i == 0:
                near, far = zrecv[way, 0, 0:1], zrecv[way, 1, 0:1]
                edge[way] = near
            span = jnp.exp(-own_rates[i] * (2 * BLK))
            row_span = jnp.exp(-own_rates[i] * (2 * BLK * ROW)) * (near == far).astype(F32)
            rows = slice(8 + i * width, 8 + (i + 1) * width)
            entering = zrecv[way, 0, rows] + row_span * zrecv[way, 1, rows]
            keep = jnp.ones((1, DH), F32)
            there_end = near
            for n in range(ROW):
                j = order[n]
                if n == 0:
                    slices[way, i, j] = entering
                else:
                    slices[way, i, j] = slices[way, i, j] + keep * entering
                here = end_of(way, j)
                keep = keep * span * (here == there_end).astype(F32)
                there_end = here
            mine = pl.ds(pl.multiple_of(y * width, width), width)
            raw[way, i, mine] = slices[way, i, y]
            for n, j in enumerate(in_row):
                sends.append(
                    copy(
                        slices.at[way, i, j],
                        raw.at[way, i, mine],
                        b_send.at[way, i, n],
                        b_recv.at[way, i, y],
                        at(z, j, c),
                    )
                )
                sends[-1].start()

    to_chips(0)
    to_chips(1)

    beside = []
    for way in (0, 1):
        neighbour = rmeta[(y + ROW - 1) % ROW, 1:2, :] if way == 0 else rmeta[(y + 1) % ROW, 0:1, :]
        beside.append(jnp.where(y == (0 if way == 0 else ROW - 1), edge[way], neighbour))

    def to_core(way):
        inner = lasts[0] if way == 0 else firsts[1]
        kept = (inner == beside[way]).astype(F32)
        for i in range(OWN):
            for j in in_row:
                theirs = pl.ds(pl.multiple_of(j * width, width), width)
                copy(
                    slices.at[way, i, j], raw.at[way, i, theirs], b_send.at[way, i, 0], b_recv.at[way, i, j], partner
                ).wait_recv()
            outer = raw[way, i]
            between = jnp.where(c == way, local[way, OWN * c + i], part[way, i])
            inside = between + jnp.exp(-own_rates[i] * BLK) * kept * outer
            state[way, OWN * c + i] = jnp.where(c == way, outer, inside)
            give[way, i] = jnp.where(c == way, inside, outer)
            sends.append(
                copy(
                    give.at[way, i],
                    state.at[way, OWN * c + i],
                    e_send.at[way, i],
                    e_recv.at[way, i],
                    partner,
                )
            )
            sends[-1].start()

    def from_core(way):
        for i in range(OWN):
            copy(
                give.at[way, i], state.at[way, OWN * (1 - c) + i], e_send.at[way, i], e_recv.at[way, i], partner
            ).wait_recv()

    to_core(0)
    from_core(0)

    seg_before = jnp.where(c == 0, beside[0], lasts[0])
    seg_after = jnp.where(c == 1, beside[1], firsts[1])
    joins = (seg_cols == seg_before).astype(F32)
    leaves = (seg_cols == seg_after).astype(F32)

    squares = None
    for h in range(NH):
        inflow = jnp.exp(-rates[h] * (place + 1.0)) * joins
        high, low = split(state[0, h])
        qh = q[:, cols[h]]
        whole = out[:, cols[h]] + inflow * (dot(qh, high, NN) + dot(qh, low, NN))
        out[:, cols[h]] = whole
        squares = whole * whole if h == 0 else squares + whole * whole
    mine = jnp.broadcast_to(jnp.sum(squares.T, axis=0, keepdims=True), (8, DH))
    xsend[...] = mine
    xrecv[x] = mine
    for n in range(1, xs):
        sends.append(copy(xsend, xrecv.at[x], x_send.at[n - 1], x_recv.at[x], (s, (x + n) % xs)))
        sends[-1].start()

    to_core(1)
    for h in range(NH):
        inflow = jnp.exp(-rates[h] * (place + 1.0)) * joins
        high, low = split(state[0, h])
        gh = g[:, cols[h]]
        dq[:, cols[h]] = dq[:, cols[h]] + inflow * (dot(gh, high, NT) + dot(gh, low, NT))
    from_core(1)
    for h in range(NH):
        outflow = jnp.exp(-rates[h] * (BLK - place)) * leaves
        high, low = split(state[1, h])
        kh, vh = k[:, cols[h]], v[:, cols[h]]
        dk[:, cols[h]] = dk[:, cols[h]] + outflow * (dot(vh, high, NT) + dot(vh, low, NT))
        dv[:, cols[h]] = dv[:, cols[h]] + outflow * (dot(kh, high, NN) + dot(kh, low, NN))

    for n in range(1, xs):
        from_x = (x + n) % xs
        copy(xsend, xrecv.at[from_x], x_send.at[n - 1], x_recv.at[from_x], partner).wait_recv()
    summed = xrecv[0]
    for n in range(1, xs):
        summed = summed + xrecv[n]
    inverse = lax.rsqrt(summed / (NH * DH * xs) + EPSILON)
    scale = jnp.broadcast_to(inverse[0:1, :], (BLK, BLK)).T
    for h in range(NH):
        normed[:, cols[h]] = out[:, cols[h]] * scale * gain[:, cols[h]]

    for sent in sends:
        sent.wait_send()
    for w, n in hops:
        for i in range(OWN):

            @pl.when(after(w) >= n)
            def _():
                z_copy(w, n, i).wait_send()


def finish(*refs):
    sems = refs[8]
    stores = [pltpu.make_async_copy(refs[n], refs[4 + n], sems.at[n]) for n in range(4)]
    for store in stores:
        store.start()
    for store in stores:
        store.wait()


def body(zs, xs, queries, keys, values, d_out, segment_ids, decay_exps, gain):
    width = BLK // ROW
    vmem = pl.BlockSpec(memory_space=pltpu.VMEM)
    dma = pltpu.SemaphoreType.DMA
    result = jax.ShapeDtypeStruct((BLK, NH * DH), F32)
    operands = (
        decay_exps, segment_ids.reshape(1, BLK), queries, keys, values, d_out, gain.reshape(1, NH * DH)
    )
    held = pl.pallas_call(
        functools.partial(kernel, zs, xs),
        out_shape=(result,) * 4,
        in_specs=[pl.BlockSpec(memory_space=pltpu.HBM)] * 7,
        out_specs=(vmem,) * 4,
        scratch_shapes=[
            pltpu.SMEM((NH,), jnp.int32),
            pltpu.VMEM((1, BLK), jnp.int32),
            *[pltpu.VMEM((BLK, NH * DH), BF16)] * 4,
            pltpu.VMEM((1, NH * DH), F32),
            pltpu.VMEM((2, NH, DH, DH), F32),
            pltpu.VMEM((2, OWN, DH, DH), F32),
            pltpu.VMEM((8, DH), F32),
            pltpu.VMEM((8, DH), F32),
            pltpu.VMEM((2, OWN, DH, DH), F32),
            pltpu.VMEM((8, DH), F32),
            pltpu.VMEM((ROW, 8, DH), F32),
            pltpu.VMEM((2, OWN, ROW, width, DH), F32),
            pltpu.VMEM((2, 8 + OWN * width, DH), F32),
            pltpu.VMEM((2, 2, 8 + OWN * width, DH), F32),
            pltpu.VMEM((2, OWN, ROW, width, DH), F32),
            pltpu.VMEM((2, OWN, DH, DH), F32),
            pltpu.VMEM((2, OWN, DH, DH), F32),
            pltpu.VMEM((2, NH, DH, DH), F32),
            pltpu.VMEM((BLK, NH * DH), F32),
            pltpu.VMEM((8, DH), F32),
            pltpu.VMEM((xs, 8, DH), F32),
            dma((7,)),
            dma((2, OWN)), dma((2, OWN)),
            dma((1 + ROW,)), dma((1 + ROW,)),
            dma((2, OWN, ROW)), dma((2, OWN, ROW)),
            dma((2, 2, OWN)), dma((2, 2, OWN)),
            dma((2, OWN, ROW)), dma((2, OWN, ROW)),
            dma((2, OWN)), dma((2, OWN)),
            dma((xs,)), dma((xs,)),
        ],
        compiler_params=pltpu.CompilerParams(
            collective_id=0, has_side_effects=True, vmem_limit_bytes=32 << 20
        ),
        name="attention",
    )(*(pltpu.with_memory_space_constraint(operand, pltpu.HBM) for operand in operands))
    return pl.pallas_call(
        finish,
        out_shape=(result,) * 4,
        in_specs=[vmem] * 4,
        out_specs=(pl.BlockSpec(memory_space=pl.ANY),) * 4,
        scratch_shapes=[dma((4,))],
        name="finish",
    )(*(pltpu.with_memory_space_constraint(part, pltpu.VMEM) for part in held))


def solution(mesh):
    both = P("seq", "head")
    return jax.shard_map(
        functools.partial(body, mesh.shape["seq"] // (2 * ROW), mesh.shape["head"]),
        mesh=mesh,
        in_specs=(both, both, both, both, P("seq"), P("head"), P("head")),
        out_specs=(both, both, both, both),
        check_vma=False,
    )
```

```python
import functools

import jax
import jax.numpy as jnp
from jax import lax
from jax.experimental import pallas as pl
from jax.experimental.pallas import tpu as pltpu
from jax.sharding import PartitionSpec as P

DH = 128
BLK = 128
NH = 4
OWN = 2
ROW = 8
PIECES = 1
EPSILON = 1e-06
MESH = pl.DeviceIdType.MESH
F32 = jnp.float32
BF16 = jnp.bfloat16

NN = (((1,), (0,)), ((), ()))
NT = (((1,), (1,)), ((), ()))
TN = (((0,), (0,)), ((), ()))


def dot(a, b, dims):
    return lax.dot_general(a, b, dims, preferred_element_type=F32)


def split(a):
    high = a.astype(BF16)
    return high, (a - high.astype(F32)).astype(BF16)


def kernel(
    zs, xs, exps_in, seg_in, q_in, k_in, v_in, g_in, gain_in,
    normed, dq, dk, dv,
    exps, seg, q, k, v, g, gain,
    local, part, mymeta, pmeta, chip, cmeta, rmeta, there, zsend, zrecv, slices, raw, give, state, out, inw, outw,
    given, got, pout, outgot, xsend, xrecv,
    loads, g_send, g_recv, o_send, o_recv, d_send, d_recv, m_send, m_recv, t_send, t_recv, z_send, z_recv, b_send, b_recv, e_send, e_recv, x_send, x_recv,
):
    s, x = lax.axis_index("seq"), lax.axis_index("head")
    c, y, z = s % 2, (s // 2) % ROW, s // (2 * ROW)
    width = BLK // ROW
    total_tokens = BLK * 2 * ROW * zs

    def at(zz, yy, cc):
        return ((zz * ROW + yy) * 2 + cc, x)

    partner = at(z, y, 1 - c)
    far_first = sorted(range(1, ROW), key=lambda n: -min(n, ROW - n))
    in_row = [(y + n) % ROW for n in far_first]
    x_first = sorted(range(1, xs), key=lambda n: -min(n, xs - n))

    def hop(way, n):
        return at((z + (n if way == 0 else zs - n)) % zs, y, c)

    def copy(src, dst, send, recv, device):
        return pltpu.make_async_remote_copy(
            src_ref=src, dst_ref=dst, send_sem=send, recv_sem=recv, device_id=device, device_id_type=MESH
        )

    def after(way):
        return zs - 1 - z if way == 0 else z

    def before(way):
        return after(1 - way)

    halves = [pl.ds(pl.multiple_of(OWN * DH * n, OWN * DH), OWN * DH) for n in (1 - c, c)]
    fetches = [
        pltpu.make_async_copy(src, dst, loads.at[n])
        for n, (src, dst) in enumerate(
            [(seg_in, seg), (exps_in, exps)]
            + [(ref.at[:, half], to.at[:, half]) for half in halves for ref, to in ((k_in, k), (v_in, v))]
            + [(q_in, q), (g_in, g), (gain_in, gain)]
        )
    ]
    for fetch in fetches:
        fetch.start()
    barrier = pltpu.get_barrier_semaphore()
    others = [at(z, j, c) for j in in_row] + [(s, (x + n) % xs) for n in x_first]
    others += [(partner[0], (x + n) % xs) for n in x_first] + [partner]
    for device in others:
        pl.semaphore_signal(barrier, inc=1, device_id=device, device_id_type=MESH)
    hops = [(w, n) for w in (0, 1) for n in (1, 2)]
    for w, n in hops:

        @pl.when(after(w) >= n)
        def _():
            pl.semaphore_signal(barrier, inc=1, device_id=hop(w, n), device_id_type=MESH)

    for w, n in hops:

        @pl.when(before(w) < n)
        def _():
            zrecv[w, n - 1, 0:8] = jnp.full((8, DH), -float(n), F32)
            zrecv[w, n - 1, 8:] = jnp.zeros((OWN * width, DH), F32)

    for fetch in fetches[:2]:
        fetch.wait()

    place = lax.broadcasted_iota(jnp.int32, (BLK, DH), 0).astype(F32)
    seg_row = seg[...].astype(F32)
    seg_rows = jnp.broadcast_to(seg_row, (BLK, BLK))
    seg_cols = seg_rows.T
    first = jnp.broadcast_to(seg_cols[0:1, :], (8, DH))
    last = jnp.broadcast_to(seg_cols[BLK - 1 : BLK, :], (8, DH))
    row_id = lax.broadcasted_iota(jnp.int32, (8, DH), 0)
    mymeta[...] = jnp.where(row_id == 0, first, jnp.where(row_id == 1, last, seg_rows[0:8]))

    def rate_of(h):
        whole = jnp.left_shift(jnp.ones((1, DH), jnp.int32), jnp.full((1, DH), exps[h], jnp.int32))
        return whole.astype(F32) / total_tokens

    rates = [rate_of(h) for h in range(NH)]
    own_rates = [rate_of(OWN * c + i) for i in range(OWN)]
    cols = [slice(h * DH, (h + 1) * DH) for h in range(NH)]

    def weighted(weight, left, right):
        high, low = split(weight * left.astype(F32))
        return dot(high, right, TN) + dot(low, right, TN)

    ends = (seg_cols == last[0:1, :]).astype(F32)
    starts = (seg_cols == first[0:1, :]).astype(F32)
    mine = [OWN * c + i for i in range(OWN)]
    theirs = [OWN * (1 - c) + i for i in range(OWN)]
    their_rates = [rate_of(h) for h in theirs]

    def columns(h):
        return pl.ds(pl.multiple_of(h * DH, DH), DH)

    def local_state(way, h, rate):
        if way == 0:
            weight = jnp.exp(-rate * (BLK - 1.0 - place)) * ends
            local[0, h] = weighted(weight, k[:, columns(h)], v[:, columns(h)])
        else:
            weight = jnp.exp(-rate * place) * starts
            local[1, h] = weighted(weight, q[:, columns(h)], g[:, columns(h)])

    distance = place - lax.broadcasted_iota(jnp.int32, (BLK, DH), 1).astype(F32)
    causal = (distance >= 0) & (seg_cols == seg_rows)
    reach = jnp.maximum(distance, 0.0)

    def within(h):
        decay = jnp.where(causal, jnp.exp(-rates[h] * reach), 0.0)
        qh, kh, vh, gh = q[:, cols[h]], k[:, cols[h]], v[:, cols[h]], g[:, cols[h]]
        scores = (dot(qh, kh, NT) * decay).astype(BF16)
        grad_scores = (dot(gh, vh, NT) * decay).astype(BF16)
        out[:, cols[h]] = dot(scores, vh, NN)
        dq[:, cols[h]] = dot(grad_scores, kh, NN)
        dk[:, cols[h]] = dot(grad_scores, qh, TN)
        dv[:, cols[h]] = dot(scores, gh, TN)

    def in_blocks():
        for h in range(NH):
            within(h)
        given[...] = q[:, halves[0]].astype(F32)

    def wait_for(some):
        for fetch in some:
            fetch.wait()

    def local_states(way, heads, head_rates):
        for h, rate in zip(heads, head_rates):
            local_state(way, h, rate)

    last_out = (s == 0) & (x == 0)

    @pl.when(last_out)
    def _():
        wait_for(fetches[2:4])
        local_states(0, theirs, their_rates)

    @pl.when(jnp.logical_not(last_out))
    def _():
        wait_for(fetches[2:])
        for way in (0, 1):
            local_states(way, theirs, their_rates)
            local_states(way, mine, own_rates)
        in_blocks()

    pl.semaphore_wait(barrier, len(others) + jnp.minimum(z, 2) + jnp.minimum(zs - 1 - z, 2))

    meta_copy = copy(mymeta, pmeta, m_send.at[0], m_recv.at[0], partner)
    meta_copy.start()
    sends = [meta_copy]

    first_copies = [
        [
            copy(local.at[way, theirs[i]], part.at[way, i], d_send.at[way, i], d_recv.at[way, i], partner)
            for i in range(OWN)
        ]
        for way in (0, 1)
    ]
    sends.extend(first_copies[0] + first_copies[1])
    for first_copy in first_copies[0]:
        first_copy.start()

    @pl.when(last_out)
    def _():
        wait_for(fetches[4:6])
        local_states(0, mine, own_rates)

    @pl.when(jnp.logical_not(last_out))
    def _():
        for first_copy in first_copies[1]:
            first_copy.start()


    meta_copy.wait_recv()
    firsts = [jnp.where(c == 0, mymeta[0:1, :], pmeta[0:1, :]), jnp.where(c == 0, pmeta[0:1, :], mymeta[0:1, :])]
    lasts = [jnp.where(c == 0, mymeta[1:2, :], pmeta[1:2, :]), jnp.where(c == 0, pmeta[1:2, :], mymeta[1:2, :])]
    chip_meta = jnp.where(row_id == 0, jnp.broadcast_to(firsts[0], (8, DH)), jnp.broadcast_to(lasts[1], (8, DH)))
    cmeta[...] = chip_meta
    rmeta[y] = chip_meta
    same_chip = [(lasts[0] == lasts[1]).astype(F32), (firsts[0] == firsts[1]).astype(F32)]

    def to_row(way):
        for i in range(OWN):
            first_copies[way][i].wait_recv()
            carried = jnp.exp(-own_rates[i] * BLK) * same_chip[way]
            mine = jnp.where(c == 1 - way, 1.0, carried)
            theirs = jnp.where(c == 1 - way, carried, 1.0)
            whole = mine * local[way, OWN * c + i] + theirs * part[way, i]
            chip[way, i] = whole
            for n, j in enumerate(in_row):
                sends.append(
                    copy(
                        chip.at[way, i, pl.ds(pl.multiple_of(j * width, width), width)],
                        there.at[way, i, y],
                        t_send.at[way, i, n],
                        t_recv.at[way, i, y],
                        at(z, j, c),
                    )
                )
                sends[-1].start()
            there[way, i, y] = chip[way, i, pl.ds(pl.multiple_of(y * width, width), width), :]

    to_row(0)
    for n, j in enumerate(in_row):
        sends.append(copy(cmeta, rmeta.at[y], m_send.at[1 + n], m_recv.at[1 + y], at(z, j, c)))
        sends[-1].start()

    @pl.when(last_out)
    def _():
        wait_for(fetches[6:])
        local_states(1, theirs, their_rates)
        for first_copy in first_copies[1]:
            first_copy.start()
        local_states(1, mine, own_rates)


    to_row(1)

    @pl.when(last_out)
    def _():
        in_blocks()

    gifts = [
        copy(given, got.at[0], g_send.at[0], g_recv.at[0], partner),
        copy(out.at[:, halves[0]], got.at[1], g_send.at[1], g_recv.at[1], partner),
    ]
    for gift in gifts:
        gift.start()
    sends.extend(gifts)

    for j in in_row:
        copy(cmeta, rmeta.at[j], m_send.at[0], m_recv.at[1 + j], partner).wait_recv()

    def end_of(way, j):
        return rmeta[j, 1:2, :] if way == 0 else rmeta[j, 0:1, :]

    def z_copy(way, n, i):
        rows = slice(0, 8 + width) if i == 0 else slice(8 + width, 8 + 2 * width)
        return copy(
            zsend.at[way, rows], zrecv.at[way, n - 1, rows], z_send.at[way, n - 1, i], z_recv.at[way, n - 1, i], hop(way, n)
        )

    orders = [list(range(ROW)), list(range(ROW))[::-1]]

    def row_copy(way, i, j):
        return copy(there.at[way, i, y], there.at[way, i, j], t_send.at[way, i, 0], t_recv.at[way, i, j], partner)

    def end_wait(way, i):
        end = orders[way][-1]

        @pl.when(y != end)
        def _():
            row_copy(way, i, end).wait_recv()

    def to_rows(way):
        order = orders[way]
        zsend[way, 0:8] = jnp.broadcast_to(end_of(way, order[-1]), (8, DH))
        for i in range(OWN):
            for j in in_row:

                @pl.when(j != order[-1])
                def _():
                    row_copy(way, i, j).wait_recv()

            span = jnp.exp(-own_rates[i] * (2 * BLK))
            sofar = there[way, i, order[0]]
            for n in range(1, ROW):
                slices[way, i, order[n]] = sofar
                keep = span * (end_of(way, order[n]) == end_of(way, order[n - 1])).astype(F32)
                if n < ROW - 1:
                    sofar = there[way, i, order[n]] + keep * sofar

            @pl.when(after(way) >= 1)
            def _():
                end_wait(way, i)
                zsend[way, 8 + i * width : 8 + (i + 1) * width] = there[way, i, order[-1]] + keep * sofar
                z_copy(way, 1, i).start()

            @pl.when(after(way) >= 2)
            def _():
                z_copy(way, 2, i).start()


    to_rows(0)
    to_rows(1)

    edge = [None, None]

    def to_chips(way):
        order = orders[way]
        for i in range(OWN):
            for n in (1, 2):

                @pl.when(before(way) >= n)
                def _():
                    z_copy(way, n, i).wait_recv()

            if i == 0:
                near, far = zrecv[way, 0, 0:1], zrecv[way, 1, 0:1]
                edge[way] = near
            span = jnp.exp(-own_rates[i] * (2 * BLK))
            row_span = jnp.exp(-own_rates[i] * (2 * BLK * ROW)) * (near == far).astype(F32)
            rows = slice(8 + i * width, 8 + (i + 1) * width)
            entering = zrecv[way, 0, rows] + row_span * zrecv[way, 1, rows]
            keep = jnp.ones((1, DH), F32)
            there_end = near
            for n in range(ROW):
                j = order[n]
                if n == 0:
                    slices[way, i, j] = entering
                else:
                    slices[way, i, j] = slices[way, i, j] + keep * entering
                here = end_of(way, j)
                keep = keep * span * (here == there_end).astype(F32)
                there_end = here
            here = pl.ds(pl.multiple_of(y * width, width), width)
            for n, j in enumerate(in_row):
                sends.append(
                    copy(
                        slices.at[way, i, j],
                        raw.at[way, i, here],
                        b_send.at[way, i, n],
                        b_recv.at[way, i, y],
                        at(z, j, c),
                    )
                )
                sends[-1].start()
            raw[way, i, here] = slices[way, i, y]

    to_chips(0)
    to_chips(1)

    beside = []
    for way in (0, 1):
        neighbour = rmeta[(y + ROW - 1) % ROW, 1:2, :] if way == 0 else rmeta[(y + 1) % ROW, 0:1, :]
        beside.append(jnp.where(y == (0 if way == 0 else ROW - 1), edge[way], neighbour))

    def to_core(way):
        inner = lasts[0] if way == 0 else firsts[1]
        kept = (inner == beside[way]).astype(F32)
        for i in range(OWN):
            for j in in_row:
                there_rows = pl.ds(pl.multiple_of(j * width, width), width)
                copy(
                    slices.at[way, i, j], raw.at[way, i, there_rows], b_send.at[way, i, 0], b_recv.at[way, i, j], partner
                ).wait_recv()
            outer = raw[way, i]
            between = jnp.where(c == way, local[way, OWN * c + i], part[way, i])
            inside = between + jnp.exp(-own_rates[i] * BLK) * kept * outer
            give[way, i] = jnp.where(c == way, inside, outer)
            sends.append(
                copy(
                    give.at[way, i],
                    state.at[way, OWN * c + i],
                    e_send.at[way, i],
                    e_recv.at[way, i],
                    partner,
                )
            )
            sends[-1].start()
            state[way, OWN * c + i] = jnp.where(c == way, outer, inside)

    def from_core(way):
        for i in range(OWN):
            copy(
                give.at[way, i], state.at[way, OWN * (1 - c) + i], e_send.at[way, i], e_recv.at[way, i], partner
            ).wait_recv()

    seg_before = jnp.where(c == 0, beside[0], lasts[0])
    seg_after = jnp.where(c == 1, beside[1], firsts[1])
    joins = (seg_cols == seg_before).astype(F32)
    leaves = (seg_cols == seg_after).astype(F32)
    partner_cols = jnp.broadcast_to(pmeta[2:3, :], (BLK, BLK)).T
    partner_joins = (partner_cols == jnp.where(c == 1, beside[0], lasts[0])).astype(F32)
    for i in range(OWN):
        weight = jnp.exp(-own_rates[i] * (place + 1.0))
        inw[0, i] = weight * joins
        inw[1, i] = weight * partner_joins
        inw[2, i] = jnp.exp(-their_rates[i] * (place + 1.0)) * joins
        outw[0, i] = jnp.exp(-own_rates[i] * (BLK - place)) * leaves
        outw[1, i] = jnp.exp(-their_rates[i] * (BLK - place)) * leaves
    for gift in gifts:
        gift.wait_recv()

    to_core(0)

    def output(within_out, query, entering, weight):
        high, low = split(entering)
        return within_out + weight * (dot(query, high, NN) + dot(query, low, NN))

    squares, partner_squares = jnp.zeros((BLK, DH), F32), jnp.zeros((BLK, DH), F32)
    for i in range(OWN):
        whole = output(got[1, :, cols[i]], got[0, :, cols[i]].astype(BF16), give[0, i], inw[1, i])
        pout[:, cols[i]] = whole
        partner_squares = partner_squares + whole * whole
        at_mine = columns(mine[i])
        whole = output(out[:, at_mine], q[:, at_mine], state[0, mine[i]], inw[0, i])
        out[:, at_mine] = whole
        squares = squares + whole * whole

    def row_of(total):
        return jnp.broadcast_to(jnp.sum(total.T, axis=0, keepdims=True), (8, DH))

    xsend[0] = row_of(squares)
    xsend[1] = row_of(partner_squares)
    last_sends = [
        copy(xsend.at[m], xrecv.at[c, x], x_send.at[m, n], x_recv.at[c, x], (to, (x + n) % xs))
        for n in x_first
        for m, to in ((0, s), (1, partner[0]))
    ]
    last_sends.append(copy(xsend.at[1], xrecv.at[c, x], x_send.at[1, 0], x_recv.at[c, x], partner))
    for sent in last_sends:
        sent.start()
    out_copy = copy(pout, outgot, o_send.at[0], o_recv.at[0], partner)
    out_copy.start()
    sends.append(out_copy)
    xrecv[c, x] = xsend[0]

    to_core(1)

    def grad_query(h, inflow):
        high, low = split(state[0, h])
        gh = g[:, columns(h)]
        dq[:, columns(h)] = dq[:, columns(h)] + inflow * (dot(gh, high, NT) + dot(gh, low, NT))

    def grad_key_value(h, outflow):
        high, low = split(state[1, h])
        kh, vh = k[:, columns(h)], v[:, columns(h)]
        dk[:, columns(h)] = dk[:, columns(h)] + outflow * (dot(vh, high, NT) + dot(vh, low, NT))
        dv[:, columns(h)] = dv[:, columns(h)] + outflow * (dot(kh, high, NN) + dot(kh, low, NN))

    for i in range(OWN):
        grad_key_value(mine[i], outw[0, i])
        grad_query(mine[i], inw[0, i])
    from_core(0)
    for i in range(OWN):
        grad_query(theirs[i], inw[2, i])
    from_core(1)
    for i in range(OWN):
        grad_key_value(theirs[i], outw[1, i])

    for way in (0, 1):

        @pl.when(after(way) < 1)
        def _():
            for i in range(OWN):
                end_wait(way, i)

    out_copy.wait_recv()
    for sent in sends:
        sent.wait_send()
    for w, n in hops:
        for i in range(OWN):

            @pl.when(after(w) >= n)
            def _():
                z_copy(w, n, i).wait_send()

    for m in (c, 1 - c):
        for n in (x_first if m is c else [*x_first, 0]):
            from_x = (x + n) % xs
            copy(xsend.at[0], xrecv.at[m, from_x], x_send.at[0, n], x_recv.at[m, from_x], partner).wait_recv()
    summed = xrecv[0, 0] + xrecv[1, 0]
    for n in range(1, xs):
        summed = summed + (xrecv[0, n] + xrecv[1, n])
    inverse = lax.rsqrt(summed / (NH * DH * xs) + EPSILON)
    scale = jnp.broadcast_to(inverse[0:1, :], (BLK, BLK)).T
    for i in range(OWN):
        at_mine, at_theirs = columns(mine[i]), columns(theirs[i])
        normed[:, at_mine] = out[:, at_mine] * gain[:, at_mine] * scale
        normed[:, at_theirs] = outgot[:, cols[i]] * gain[:, at_theirs] * scale
    for sent in last_sends:
        sent.wait_send()


def finish(*refs):
    sems = refs[8]
    rows = [pl.ds(n * BLK // PIECES, BLK // PIECES) for n in range(PIECES)]
    stores = [
        pltpu.make_async_copy(refs[n].at[piece], refs[4 + n].at[piece], sems.at[n, m])
        for n in range(4)
        for m, piece in enumerate(rows)
    ]
    for store in stores:
        store.start()
    for store in stores:
        store.wait()


def body(zs, xs, queries, keys, values, d_out, segment_ids, decay_exps, gain):
    width = BLK // ROW
    vmem = pl.BlockSpec(memory_space=pltpu.VMEM)
    dma = pltpu.SemaphoreType.DMA
    result = jax.ShapeDtypeStruct((BLK, NH * DH), F32)
    operands = (
        decay_exps, segment_ids.reshape(1, BLK), queries, keys, values, d_out, gain.reshape(1, NH * DH)
    )
    held = pl.pallas_call(
        functools.partial(kernel, zs, xs),
        out_shape=(result,) * 4,
        in_specs=[pl.BlockSpec(memory_space=pltpu.HBM)] * 7,
        out_specs=(vmem,) * 4,
        scratch_shapes=[
            pltpu.SMEM((NH,), jnp.int32),
            pltpu.VMEM((1, BLK), jnp.int32),
            *[pltpu.VMEM((BLK, NH * DH), BF16)] * 4,
            pltpu.VMEM((1, NH * DH), F32),
            pltpu.VMEM((2, NH, DH, DH), F32),
            pltpu.VMEM((2, OWN, DH, DH), F32),
            pltpu.VMEM((8, DH), F32),
            pltpu.VMEM((8, DH), F32),
            pltpu.VMEM((2, OWN, DH, DH), F32),
            pltpu.VMEM((8, DH), F32),
            pltpu.VMEM((ROW, 8, DH), F32),
            pltpu.VMEM((2, OWN, ROW, width, DH), F32),
            pltpu.VMEM((2, 8 + OWN * width, DH), F32),
            pltpu.VMEM((2, 2, 8 + OWN * width, DH), F32),
            pltpu.VMEM((2, OWN, ROW, width, DH), F32),
            pltpu.VMEM((2, OWN, DH, DH), F32),
            pltpu.VMEM((2, OWN, DH, DH), F32),
            pltpu.VMEM((2, NH, DH, DH), F32),
            pltpu.VMEM((BLK, NH * DH), F32),
            pltpu.VMEM((3, OWN, BLK, DH), F32),
            pltpu.VMEM((2, OWN, BLK, DH), F32),
            pltpu.VMEM((BLK, OWN * DH), F32),
            pltpu.VMEM((2, BLK, OWN * DH), F32),
            pltpu.VMEM((BLK, OWN * DH), F32),
            pltpu.VMEM((BLK, OWN * DH), F32),
            pltpu.VMEM((2, 8, DH), F32),
            pltpu.VMEM((2, xs, 8, DH), F32),
            dma((9,)),
            dma((2,)), dma((2,)),
            dma((1,)), dma((1,)),
            dma((2, OWN)), dma((2, OWN)),
            dma((1 + ROW,)), dma((1 + ROW,)),
            dma((2, OWN, ROW)), dma((2, OWN, ROW)),
            dma((2, 2, OWN)), dma((2, 2, OWN)),
            dma((2, OWN, ROW)), dma((2, OWN, ROW)),
            dma((2, OWN)), dma((2, OWN)),
            dma((2, xs)), dma((2, xs)),
        ],
        compiler_params=pltpu.CompilerParams(
            collective_id=0, has_side_effects=True, vmem_limit_bytes=32 << 20
        ),
        name="attention",
    )(*(pltpu.with_memory_space_constraint(operand, pltpu.HBM) for operand in operands))
    return pl.pallas_call(
        finish,
        out_shape=(result,) * 4,
        in_specs=[vmem] * 4,
        out_specs=(pl.BlockSpec(memory_space=pl.ANY),) * 4,
        scratch_shapes=[dma((4, PIECES))],
        name="finish",
    )(*(pltpu.with_memory_space_constraint(part, pltpu.VMEM) for part in held))


def solution(mesh):
    both = P("seq", "head")
    return jax.shard_map(
        functools.partial(body, mesh.shape["seq"] // (2 * ROW), mesh.shape["head"]),
        mesh=mesh,
        in_specs=(both, both, both, both, P("seq"), P("head"), P("head")),
        out_specs=(both, both, both, both),
        check_vma=False,
    )
```

```python
import functools

import jax
import jax.numpy as jnp
from jax import lax
from jax.experimental import pallas as pl
from jax.experimental.pallas import tpu as pltpu
from jax.sharding import PartitionSpec as P

DH = 128
BLK = 128
NH = 4
OWN = 2
ROW = 8
PIECES = 1
EPSILON = 1e-06
MESH = pl.DeviceIdType.MESH
F32 = jnp.float32
BF16 = jnp.bfloat16

NN = (((1,), (0,)), ((), ()))
NT = (((1,), (1,)), ((), ()))
TN = (((0,), (0,)), ((), ()))


def dot(a, b, dims):
    return lax.dot_general(a, b, dims, preferred_element_type=F32)


def split(a):
    high = a.astype(BF16)
    return high, (a - high.astype(F32)).astype(BF16)


def kernel(
    zs, xs, exps_in, seg_in, q_in, k_in, v_in, g_in, gain_in,
    normed, dq, dk, dv,
    exps, seg, q, k, v, g, gain,
    local, part, mymeta, pmeta, chip, cmeta, rmeta, there, zsend, zrecv, slices, raw, give, state, out, inw, outw,
    given, got, pout, outgot, xsend, xrecv,
    loads, g_send, g_recv, o_send, o_recv, d_send, d_recv, m_send, m_recv, t_send, t_recv, z_send, z_recv, b_send, b_recv, e_send, e_recv, x_send, x_recv,
):
    s, x = lax.axis_index("seq"), lax.axis_index("head")
    c, y, z = s % 2, (s // 2) % ROW, s // (2 * ROW)
    width = BLK // ROW
    total_tokens = BLK * 2 * ROW * zs

    def at(zz, yy, cc):
        return ((zz * ROW + yy) * 2 + cc, x)

    partner = at(z, y, 1 - c)
    far_first = sorted(range(1, ROW), key=lambda n: -min(n, ROW - n))
    in_row = [(y + n) % ROW for n in far_first]
    x_first = sorted(range(1, xs), key=lambda n: -min(n, xs - n))

    def hop(way, n):
        return at((z + (n if way == 0 else zs - n)) % zs, y, c)

    def copy(src, dst, send, recv, device):
        return pltpu.make_async_remote_copy(
            src_ref=src, dst_ref=dst, send_sem=send, recv_sem=recv, device_id=device, device_id_type=MESH
        )

    def after(way):
        return zs - 1 - z if way == 0 else z

    def before(way):
        return after(1 - way)

    halves = [pl.ds(pl.multiple_of(OWN * DH * n, OWN * DH), OWN * DH) for n in (1 - c, c)]
    fetches = [
        pltpu.make_async_copy(src, dst, loads.at[n])
        for n, (src, dst) in enumerate(
            [(seg_in, seg), (exps_in, exps)]
            + [(ref.at[:, half], to.at[:, half]) for half in halves for ref, to in ((k_in, k), (v_in, v))]
            + [(q_in, q), (g_in, g), (gain_in, gain)]
        )
    ]
    for fetch in fetches:
        fetch.start()
    barrier = pltpu.get_barrier_semaphore()
    others = [at(z, j, c) for j in in_row] + [(s, (x + n) % xs) for n in x_first]
    others += [(partner[0], (x + n) % xs) for n in x_first] + [partner]
    for device in others:
        pl.semaphore_signal(barrier, inc=1, device_id=device, device_id_type=MESH)
    hops = [(w, n) for w in (0, 1) for n in (1, 2)]
    for w, n in hops:

        @pl.when(after(w) >= n)
        def _():
            pl.semaphore_signal(barrier, inc=1, device_id=hop(w, n), device_id_type=MESH)

    for w, n in hops:

        @pl.when(before(w) < n)
        def _():
            zrecv[w, n - 1, 0:8] = jnp.full((8, DH), -float(n), F32)
            zrecv[w, n - 1, 8:] = jnp.zeros((OWN * width, DH), F32)

    for fetch in fetches[:2]:
        fetch.wait()

    place = lax.broadcasted_iota(jnp.int32, (BLK, DH), 0).astype(F32)
    seg_row = seg[...].astype(F32)
    seg_rows = jnp.broadcast_to(seg_row, (BLK, BLK))
    seg_cols = seg_rows.T
    first = jnp.broadcast_to(seg_cols[0:1, :], (8, DH))
    last = jnp.broadcast_to(seg_cols[BLK - 1 : BLK, :], (8, DH))
    row_id = lax.broadcasted_iota(jnp.int32, (8, DH), 0)
    mymeta[...] = jnp.where(row_id == 0, first, jnp.where(row_id == 1, last, seg_rows[0:8]))

    def rate_of(h):
        whole = jnp.left_shift(jnp.ones((1, DH), jnp.int32), jnp.full((1, DH), exps[h], jnp.int32))
        return whole.astype(F32) / total_tokens

    rates = [rate_of(h) for h in range(NH)]
    own_rates = [rate_of(OWN * c + i) for i in range(OWN)]
    cols = [slice(h * DH, (h + 1) * DH) for h in range(NH)]

    def weighted(weight, left, right):
        high, low = split(weight * left.astype(F32))
        return dot(high, right, TN) + dot(low, right, TN)

    ends = (seg_cols == last[0:1, :]).astype(F32)
    starts = (seg_cols == first[0:1, :]).astype(F32)
    mine = [OWN * c + i for i in range(OWN)]
    theirs = [OWN * (1 - c) + i for i in range(OWN)]
    their_rates = [rate_of(h) for h in theirs]

    def columns(h):
        return pl.ds(pl.multiple_of(h * DH, DH), DH)

    def local_state(way, h, rate):
        if way == 0:
            weight = jnp.exp(-rate * (BLK - 1.0 - place)) * ends
            local[0, h] = weighted(weight, k[:, columns(h)], v[:, columns(h)])
        else:
            weight = jnp.exp(-rate * place) * starts
            local[1, h] = weighted(weight, q[:, columns(h)], g[:, columns(h)])

    distance = place - lax.broadcasted_iota(jnp.int32, (BLK, DH), 1).astype(F32)
    causal = (distance >= 0) & (seg_cols == seg_rows)
    reach = jnp.maximum(distance, 0.0)

    def within(h):
        decay = jnp.where(causal, jnp.exp(-rates[h] * reach), 0.0)
        qh, kh, vh, gh = q[:, cols[h]], k[:, cols[h]], v[:, cols[h]], g[:, cols[h]]
        scores = (dot(qh, kh, NT) * decay).astype(BF16)
        grad_scores = (dot(gh, vh, NT) * decay).astype(BF16)
        out[:, cols[h]] = dot(scores, vh, NN)
        dq[:, cols[h]] = dot(grad_scores, kh, NN)
        dk[:, cols[h]] = dot(grad_scores, qh, TN)
        dv[:, cols[h]] = dot(scores, gh, TN)

    def in_blocks():
        for h in range(NH):
            within(h)
        given[...] = q[:, halves[0]].astype(F32)

    def wait_for(some):
        for fetch in some:
            fetch.wait()

    def local_states(way, heads, head_rates):
        for h, rate in zip(heads, head_rates):
            local_state(way, h, rate)

    last_out = (s == 0) & (x == 0)

    @pl.when(last_out)
    def _():
        wait_for(fetches[2:4])
        local_states(0, theirs, their_rates)

    @pl.when(jnp.logical_not(last_out))
    def _():
        wait_for(fetches[2:])
        for way in (0, 1):
            local_states(way, theirs, their_rates)
            local_states(way, mine, own_rates)
        in_blocks()

    pl.semaphore_wait(barrier, len(others) + jnp.minimum(z, 2) + jnp.minimum(zs - 1 - z, 2))

    meta_copy = copy(mymeta, pmeta, m_send.at[0], m_recv.at[0], partner)
    meta_copy.start()
    sends = [meta_copy]

    first_copies = [
        [
            copy(local.at[way, theirs[i]], part.at[way, i], d_send.at[way, i], d_recv.at[way, i], partner)
            for i in range(OWN)
        ]
        for way in (0, 1)
    ]
    sends.extend(first_copies[0] + first_copies[1])
    for first_copy in first_copies[0]:
        first_copy.start()

    @pl.when(last_out)
    def _():
        wait_for(fetches[4:6])
        local_states(0, mine, own_rates)

    @pl.when(jnp.logical_not(last_out))
    def _():
        for first_copy in first_copies[1]:
            first_copy.start()


    meta_copy.wait_recv()
    firsts = [jnp.where(c == 0, mymeta[0:1, :], pmeta[0:1, :]), jnp.where(c == 0, pmeta[0:1, :], mymeta[0:1, :])]
    lasts = [jnp.where(c == 0, mymeta[1:2, :], pmeta[1:2, :]), jnp.where(c == 0, pmeta[1:2, :], mymeta[1:2, :])]
    chip_meta = jnp.where(row_id == 0, jnp.broadcast_to(firsts[0], (8, DH)), jnp.broadcast_to(lasts[1], (8, DH)))
    cmeta[...] = chip_meta
    rmeta[y] = chip_meta
    same_chip = [(lasts[0] == lasts[1]).astype(F32), (firsts[0] == firsts[1]).astype(F32)]

    def row_send(way, i, n, j):
        rows = pl.ds(pl.multiple_of(j * width, width), width)
        return copy(
            chip.at[way, i, rows], there.at[way, i, y], t_send.at[way, i, n], t_recv.at[way, i, y], at(z, j, c)
        )

    def meta_send(n, j):
        return copy(cmeta, rmeta.at[y], m_send.at[1 + n], m_recv.at[1 + y], at(z, j, c))

    def back_send(way, i, n, j):
        rows = pl.ds(pl.multiple_of(y * width, width), width)
        return copy(
            slices.at[way, i, j], raw.at[way, i, rows], b_send.at[way, i, n], b_recv.at[way, i, y], at(z, j, c)
        )

    def core_send(way, i):
        return copy(give.at[way, i], state.at[way, mine[i]], e_send.at[way, i], e_recv.at[way, i], partner)

    def to_row(way):
        for i in range(OWN):
            first_copies[way][i].wait_recv()
            carried = jnp.exp(-own_rates[i] * BLK) * same_chip[way]
            mine = jnp.where(c == 1 - way, 1.0, carried)
            theirs = jnp.where(c == 1 - way, carried, 1.0)
            whole = mine * local[way, OWN * c + i] + theirs * part[way, i]
            chip[way, i] = whole
            for n, j in enumerate(in_row):
                row_send(way, i, n, j).start()
            there[way, i, y] = chip[way, i, pl.ds(pl.multiple_of(y * width, width), width), :]

    def send_meta():
        for n, j in enumerate(in_row):
            meta_send(n, j).start()

    @pl.when(z == 0)
    def _():
        to_row(0)
        send_meta()

        @pl.when(last_out)
        def _():
            wait_for(fetches[6:])
            local_states(1, theirs, their_rates)
            for first_copy in first_copies[1]:
                first_copy.start()
            local_states(1, mine, own_rates)

        to_row(1)

        @pl.when(last_out)
        def _():
            in_blocks()

    @pl.when(z != 0)
    def _():
        to_row(1)
        send_meta()
        to_row(0)

    gifts = [
        copy(given, got.at[0], g_send.at[0], g_recv.at[0], partner),
        copy(out.at[:, halves[0]], got.at[1], g_send.at[1], g_recv.at[1], partner),
    ]
    for gift in gifts:
        gift.start()
    sends.extend(gifts)

    for j in in_row:
        copy(cmeta, rmeta.at[j], m_send.at[0], m_recv.at[1 + j], partner).wait_recv()

    def end_of(way, j):
        return rmeta[j, 1:2, :] if way == 0 else rmeta[j, 0:1, :]

    def z_copy(way, n, i):
        rows = slice(0, 8 + width) if i == 0 else slice(8 + width, 8 + 2 * width)
        return copy(
            zsend.at[way, rows], zrecv.at[way, n - 1, rows], z_send.at[way, n - 1, i], z_recv.at[way, n - 1, i], hop(way, n)
        )

    orders = [list(range(ROW)), list(range(ROW))[::-1]]

    def row_copy(way, i, j):
        return copy(there.at[way, i, y], there.at[way, i, j], t_send.at[way, i, 0], t_recv.at[way, i, j], partner)

    def end_wait(way, i):
        end = orders[way][-1]

        @pl.when(y != end)
        def _():
            row_copy(way, i, end).wait_recv()

    def to_rows(way):
        order = orders[way]
        zsend[way, 0:8] = jnp.broadcast_to(end_of(way, order[-1]), (8, DH))
        for i in range(OWN):
            for j in in_row:

                @pl.when(j != order[-1])
                def _():
                    row_copy(way, i, j).wait_recv()

            span = jnp.exp(-own_rates[i] * (2 * BLK))
            sofar = there[way, i, order[0]]
            for n in range(1, ROW):
                slices[way, i, order[n]] = sofar
                keep = span * (end_of(way, order[n]) == end_of(way, order[n - 1])).astype(F32)
                if n < ROW - 1:
                    sofar = there[way, i, order[n]] + keep * sofar

            @pl.when(after(way) >= 1)
            def _():
                end_wait(way, i)
                zsend[way, 8 + i * width : 8 + (i + 1) * width] = there[way, i, order[-1]] + keep * sofar
                z_copy(way, 1, i).start()

            @pl.when(after(way) >= 2)
            def _():
                z_copy(way, 2, i).start()


    def to_chips(way):
        order = orders[way]
        for i in range(OWN):
            for n in (1, 2):

                @pl.when(before(way) >= n)
                def _():
                    z_copy(way, n, i).wait_recv()

            if i == 0:
                near, far = zrecv[way, 0, 0:1], zrecv[way, 1, 0:1]
            span = jnp.exp(-own_rates[i] * (2 * BLK))
            row_span = jnp.exp(-own_rates[i] * (2 * BLK * ROW)) * (near == far).astype(F32)
            rows = slice(8 + i * width, 8 + (i + 1) * width)
            entering = zrecv[way, 0, rows] + row_span * zrecv[way, 1, rows]
            keep = jnp.ones((1, DH), F32)
            there_end = near
            for n in range(ROW):
                j = order[n]
                if n == 0:
                    slices[way, i, j] = entering
                else:
                    slices[way, i, j] = slices[way, i, j] + keep * entering
                here = end_of(way, j)
                keep = keep * span * (here == there_end).astype(F32)
                there_end = here
            for n, j in enumerate(in_row):
                back_send(way, i, n, j).start()
            here = pl.ds(pl.multiple_of(y * width, width), width)
            raw[way, i, here] = slices[way, i, y]

    @pl.when(z == 0)
    def _():
        for way in (0, 1):
            to_rows(way)
            to_chips(way)

    @pl.when(z != 0)
    def _():
        to_rows(1)
        to_rows(0)
        to_chips(0)
        to_chips(1)

    beside = []
    for way in (0, 1):
        neighbour = rmeta[(y + ROW - 1) % ROW, 1:2, :] if way == 0 else rmeta[(y + 1) % ROW, 0:1, :]
        beside.append(jnp.where(y == (0 if way == 0 else ROW - 1), zrecv[way, 0, 0:1], neighbour))

    def to_core(way):
        inner = lasts[0] if way == 0 else firsts[1]
        kept = (inner == beside[way]).astype(F32)
        for i in range(OWN):
            for j in in_row:
                there_rows = pl.ds(pl.multiple_of(j * width, width), width)
                copy(
                    slices.at[way, i, j], raw.at[way, i, there_rows], b_send.at[way, i, 0], b_recv.at[way, i, j], partner
                ).wait_recv()
            outer = raw[way, i]
            between = jnp.where(c == way, local[way, OWN * c + i], part[way, i])
            inside = between + jnp.exp(-own_rates[i] * BLK) * kept * outer
            give[way, i] = jnp.where(c == way, inside, outer)
            core_send(way, i).start()
            state[way, OWN * c + i] = jnp.where(c == way, outer, inside)

    def from_core(way):
        for i in range(OWN):
            copy(
                give.at[way, i], state.at[way, OWN * (1 - c) + i], e_send.at[way, i], e_recv.at[way, i], partner
            ).wait_recv()

    seg_before = jnp.where(c == 0, beside[0], lasts[0])
    seg_after = jnp.where(c == 1, beside[1], firsts[1])
    joins = (seg_cols == seg_before).astype(F32)
    leaves = (seg_cols == seg_after).astype(F32)
    partner_cols = jnp.broadcast_to(pmeta[2:3, :], (BLK, BLK)).T
    partner_joins = (partner_cols == jnp.where(c == 1, beside[0], lasts[0])).astype(F32)
    for i in range(OWN):
        weight = jnp.exp(-own_rates[i] * (place + 1.0))
        inw[0, i] = weight * joins
        inw[1, i] = weight * partner_joins
        inw[2, i] = jnp.exp(-their_rates[i] * (place + 1.0)) * joins
        outw[0, i] = jnp.exp(-own_rates[i] * (BLK - place)) * leaves
        outw[1, i] = jnp.exp(-their_rates[i] * (BLK - place)) * leaves
    for gift in gifts:
        gift.wait_recv()

    to_core(0)

    def output(within_out, query, entering, weight):
        high, low = split(entering)
        return within_out + weight * (dot(query, high, NN) + dot(query, low, NN))

    squares, partner_squares = jnp.zeros((BLK, DH), F32), jnp.zeros((BLK, DH), F32)
    for i in range(OWN):
        whole = output(got[1, :, cols[i]], got[0, :, cols[i]].astype(BF16), give[0, i], inw[1, i])
        pout[:, cols[i]] = whole
        partner_squares = partner_squares + whole * whole
        at_mine = columns(mine[i])
        whole = output(out[:, at_mine], q[:, at_mine], state[0, mine[i]], inw[0, i])
        out[:, at_mine] = whole
        squares = squares + whole * whole

    def row_of(total):
        return jnp.broadcast_to(jnp.sum(total.T, axis=0, keepdims=True), (8, DH))

    xsend[0] = row_of(squares)
    xsend[1] = row_of(partner_squares)
    last_sends = [
        copy(xsend.at[m], xrecv.at[c, x], x_send.at[m, n], x_recv.at[c, x], (to, (x + n) % xs))
        for n in x_first
        for m, to in ((0, s), (1, partner[0]))
    ]
    last_sends.append(copy(xsend.at[1], xrecv.at[c, x], x_send.at[1, 0], x_recv.at[c, x], partner))
    for sent in last_sends:
        sent.start()
    out_copy = copy(pout, outgot, o_send.at[0], o_recv.at[0], partner)
    out_copy.start()
    sends.append(out_copy)
    xrecv[c, x] = xsend[0]

    to_core(1)

    def grad_query(h, inflow):
        high, low = split(state[0, h])
        gh = g[:, columns(h)]
        dq[:, columns(h)] = dq[:, columns(h)] + inflow * (dot(gh, high, NT) + dot(gh, low, NT))

    def grad_key_value(h, outflow):
        high, low = split(state[1, h])
        kh, vh = k[:, columns(h)], v[:, columns(h)]
        dk[:, columns(h)] = dk[:, columns(h)] + outflow * (dot(vh, high, NT) + dot(vh, low, NT))
        dv[:, columns(h)] = dv[:, columns(h)] + outflow * (dot(kh, high, NN) + dot(kh, low, NN))

    for i in range(OWN):
        grad_key_value(mine[i], outw[0, i])
        grad_query(mine[i], inw[0, i])
    from_core(0)
    for i in range(OWN):
        grad_query(theirs[i], inw[2, i])
    from_core(1)
    for i in range(OWN):
        grad_key_value(theirs[i], outw[1, i])

    for way in (0, 1):

        @pl.when(after(way) < 1)
        def _():
            for i in range(OWN):
                end_wait(way, i)

    out_copy.wait_recv()
    for n, j in enumerate(in_row):
        meta_send(n, j).wait_send()
    for way in (0, 1):
        for i in range(OWN):
            for n, j in enumerate(in_row):
                row_send(way, i, n, j).wait_send()
                back_send(way, i, n, j).wait_send()
            core_send(way, i).wait_send()
    for sent in sends:
        sent.wait_send()
    for w, n in hops:
        for i in range(OWN):

            @pl.when(after(w) >= n)
            def _():
                z_copy(w, n, i).wait_send()

    for m in (c, 1 - c):
        for n in (x_first if m is c else [*x_first, 0]):
            from_x = (x + n) % xs
            copy(xsend.at[0], xrecv.at[m, from_x], x_send.at[0, n], x_recv.at[m, from_x], partner).wait_recv()
    summed = xrecv[0, 0] + xrecv[1, 0]
    for n in range(1, xs):
        summed = summed + (xrecv[0, n] + xrecv[1, n])
    inverse = lax.rsqrt(summed / (NH * DH * xs) + EPSILON)
    scale = jnp.broadcast_to(inverse[0:1, :], (BLK, BLK)).T
    for i in range(OWN):
        at_mine, at_theirs = columns(mine[i]), columns(theirs[i])
        normed[:, at_mine] = out[:, at_mine] * gain[:, at_mine] * scale
        normed[:, at_theirs] = outgot[:, cols[i]] * gain[:, at_theirs] * scale
    for sent in last_sends:
        sent.wait_send()


def finish(*refs):
    sems = refs[8]
    rows = [pl.ds(n * BLK // PIECES, BLK // PIECES) for n in range(PIECES)]
    stores = [
        pltpu.make_async_copy(refs[n].at[piece], refs[4 + n].at[piece], sems.at[n, m])
        for n in range(4)
        for m, piece in enumerate(rows)
    ]
    for store in stores:
        store.start()
    for store in stores:
        store.wait()


def body(zs, xs, queries, keys, values, d_out, segment_ids, decay_exps, gain):
    width = BLK // ROW
    vmem = pl.BlockSpec(memory_space=pltpu.VMEM)
    dma = pltpu.SemaphoreType.DMA
    result = jax.ShapeDtypeStruct((BLK, NH * DH), F32)
    operands = (
        decay_exps, segment_ids.reshape(1, BLK), queries, keys, values, d_out, gain.reshape(1, NH * DH)
    )
    held = pl.pallas_call(
        functools.partial(kernel, zs, xs),
        out_shape=(result,) * 4,
        in_specs=[pl.BlockSpec(memory_space=pltpu.HBM)] * 7,
        out_specs=(vmem,) * 4,
        scratch_shapes=[
            pltpu.SMEM((NH,), jnp.int32),
            pltpu.VMEM((1, BLK), jnp.int32),
            *[pltpu.VMEM((BLK, NH * DH), BF16)] * 4,
            pltpu.VMEM((1, NH * DH), F32),
            pltpu.VMEM((2, NH, DH, DH), F32),
            pltpu.VMEM((2, OWN, DH, DH), F32),
            pltpu.VMEM((8, DH), F32),
            pltpu.VMEM((8, DH), F32),
            pltpu.VMEM((2, OWN, DH, DH), F32),
            pltpu.VMEM((8, DH), F32),
            pltpu.VMEM((ROW, 8, DH), F32),
            pltpu.VMEM((2, OWN, ROW, width, DH), F32),
            pltpu.VMEM((2, 8 + OWN * width, DH), F32),
            pltpu.VMEM((2, 2, 8 + OWN * width, DH), F32),
            pltpu.VMEM((2, OWN, ROW, width, DH), F32),
            pltpu.VMEM((2, OWN, DH, DH), F32),
            pltpu.VMEM((2, OWN, DH, DH), F32),
            pltpu.VMEM((2, NH, DH, DH), F32),
            pltpu.VMEM((BLK, NH * DH), F32),
            pltpu.VMEM((3, OWN, BLK, DH), F32),
            pltpu.VMEM((2, OWN, BLK, DH), F32),
            pltpu.VMEM((BLK, OWN * DH), F32),
            pltpu.VMEM((2, BLK, OWN * DH), F32),
            pltpu.VMEM((BLK, OWN * DH), F32),
            pltpu.VMEM((BLK, OWN * DH), F32),
            pltpu.VMEM((2, 8, DH), F32),
            pltpu.VMEM((2, xs, 8, DH), F32),
            dma((9,)),
            dma((2,)), dma((2,)),
            dma((1,)), dma((1,)),
            dma((2, OWN)), dma((2, OWN)),
            dma((1 + ROW,)), dma((1 + ROW,)),
            dma((2, OWN, ROW)), dma((2, OWN, ROW)),
            dma((2, 2, OWN)), dma((2, 2, OWN)),
            dma((2, OWN, ROW)), dma((2, OWN, ROW)),
            dma((2, OWN)), dma((2, OWN)),
            dma((2, xs)), dma((2, xs)),
        ],
        compiler_params=pltpu.CompilerParams(
            collective_id=0, has_side_effects=True, vmem_limit_bytes=32 << 20
        ),
        name="attention",
    )(*(pltpu.with_memory_space_constraint(operand, pltpu.HBM) for operand in operands))
    return pl.pallas_call(
        finish,
        out_shape=(result,) * 4,
        in_specs=[vmem] * 4,
        out_specs=(pl.BlockSpec(memory_space=pl.ANY),) * 4,
        scratch_shapes=[dma((4, PIECES))],
        name="finish",
    )(*(pltpu.with_memory_space_constraint(part, pltpu.VMEM) for part in held))


def solution(mesh):
    both = P("seq", "head")
    return jax.shard_map(
        functools.partial(body, mesh.shape["seq"] // (2 * ROW), mesh.shape["head"]),
        mesh=mesh,
        in_specs=(both, both, both, both, P("seq"), P("head"), P("head")),
        out_specs=(both, both, both, both),
        check_vma=False,
    )
```

```python
import functools

import jax
import jax.numpy as jnp
from jax import lax
from jax.experimental import pallas as pl
from jax.experimental.pallas import tpu as pltpu
from jax.sharding import PartitionSpec as P

DH = 128
BLK = 128
NH = 4
OWN = 2
ROW = 8
PIECES = 1
EPSILON = 1e-06
MESH = pl.DeviceIdType.MESH
F32 = jnp.float32
BF16 = jnp.bfloat16

NN = (((1,), (0,)), ((), ()))
NT = (((1,), (1,)), ((), ()))
TN = (((0,), (0,)), ((), ()))


def dot(a, b, dims):
    return lax.dot_general(a, b, dims, preferred_element_type=F32)


def split(a):
    high = a.astype(BF16)
    return high, (a - high.astype(F32)).astype(BF16)


def kernel(
    zs, xs, exps_in, seg_in, q_in, k_in, v_in, g_in, gain_in,
    normed, dq, dk, dv,
    exps, seg, q, k, v, g, gain,
    local, part, mymeta, pmeta, chip, cmeta, rmeta, there, zsend, zrecv, slices, raw, give, state, out, inw, outw,
    given, got, pout, outgot, xsend, xrecv,
    loads, g_send, g_recv, o_send, o_recv, d_send, d_recv, m_send, m_recv, t_send, t_recv, z_send, z_recv, b_send, b_recv, e_send, e_recv, x_send, x_recv,
):
    s, x = lax.axis_index("seq"), lax.axis_index("head")
    c, y, z = s % 2, (s // 2) % ROW, s // (2 * ROW)
    width = BLK // ROW
    total_tokens = BLK * 2 * ROW * zs

    def at(zz, yy, cc):
        return ((zz * ROW + yy) * 2 + cc, x)

    partner = at(z, y, 1 - c)
    far_first = sorted(range(1, ROW), key=lambda n: -min(n, ROW - n))
    in_row = [(y + n) % ROW for n in far_first]
    x_first = sorted(range(1, xs), key=lambda n: -min(n, xs - n))

    def hop(way, n):
        return at((z + (n if way == 0 else zs - n)) % zs, y, c)

    def copy(src, dst, send, recv, device):
        return pltpu.make_async_remote_copy(
            src_ref=src, dst_ref=dst, send_sem=send, recv_sem=recv, device_id=device, device_id_type=MESH
        )

    def after(way):
        return zs - 1 - z if way == 0 else z

    def before(way):
        return after(1 - way)

    halves = [pl.ds(pl.multiple_of(OWN * DH * n, OWN * DH), OWN * DH) for n in (1 - c, c)]
    fetches = [
        pltpu.make_async_copy(src, dst, loads.at[n])
        for n, (src, dst) in enumerate(
            [(seg_in, seg), (exps_in, exps)]
            + [(ref.at[:, half], to.at[:, half]) for half in halves for ref, to in ((k_in, k), (v_in, v))]
            + [(q_in, q), (g_in, g), (gain_in, gain)]
        )
    ]
    for fetch in fetches:
        fetch.start()
    barrier = pltpu.get_barrier_semaphore()
    others = [partner] + [at(z, j, c) for j in in_row]
    others += [(at_s, (x + n) % xs) for n in x_first for at_s in (s, partner[0])]
    hops = [(w, n) for w in (0, 1) for n in (1, 2)]
    for w, n in hops:

        @pl.when(after(w) >= n)
        def _():
            pl.semaphore_signal(barrier, inc=1, device_id=hop(w, n), device_id_type=MESH)

    for device in others:
        pl.semaphore_signal(barrier, inc=1, device_id=device, device_id_type=MESH)
    for w, n in hops:

        @pl.when(before(w) < n)
        def _():
            zrecv[w, n - 1, 0:8] = jnp.full((8, DH), -float(n), F32)
            zrecv[w, n - 1, 8:] = jnp.zeros((OWN * width, DH), F32)

    for fetch in fetches[:2]:
        fetch.wait()

    place = lax.broadcasted_iota(jnp.int32, (BLK, DH), 0).astype(F32)
    seg_row = seg[...].astype(F32)
    seg_rows = jnp.broadcast_to(seg_row, (BLK, BLK))
    seg_cols = seg_rows.T
    first = jnp.broadcast_to(seg_cols[0:1, :], (8, DH))
    last = jnp.broadcast_to(seg_cols[BLK - 1 : BLK, :], (8, DH))
    row_id = lax.broadcasted_iota(jnp.int32, (8, DH), 0)
    mymeta[...] = jnp.where(row_id == 0, first, jnp.where(row_id == 1, last, seg_rows[0:8]))

    def rate_of(h):
        whole = jnp.left_shift(jnp.ones((1, DH), jnp.int32), jnp.full((1, DH), exps[h], jnp.int32))
        return whole.astype(F32) / total_tokens

    rates = [rate_of(h) for h in range(NH)]
    own_rates = [rate_of(OWN * c + i) for i in range(OWN)]
    cols = [slice(h * DH, (h + 1) * DH) for h in range(NH)]

    def weighted(weight, left, right):
        high, low = split(weight * left.astype(F32))
        return dot(high, right, TN) + dot(low, right, TN)

    ends = (seg_cols == last[0:1, :]).astype(F32)
    starts = (seg_cols == first[0:1, :]).astype(F32)
    mine = [OWN * c + i for i in range(OWN)]
    theirs = [OWN * (1 - c) + i for i in range(OWN)]
    their_rates = [rate_of(h) for h in theirs]

    def columns(h):
        return pl.ds(pl.multiple_of(h * DH, DH), DH)

    def local_state(way, h, rate):
        if way == 0:
            weight = jnp.exp(-rate * (BLK - 1.0 - place)) * ends
            local[0, h] = weighted(weight, k[:, columns(h)], v[:, columns(h)])
        else:
            weight = jnp.exp(-rate * place) * starts
            local[1, h] = weighted(weight, q[:, columns(h)], g[:, columns(h)])

    distance = place - lax.broadcasted_iota(jnp.int32, (BLK, DH), 1).astype(F32)
    causal = (distance >= 0) & (seg_cols == seg_rows)
    reach = jnp.maximum(distance, 0.0)

    def within(h):
        decay = jnp.where(causal, jnp.exp(-rates[h] * reach), 0.0)
        qh, kh, vh, gh = q[:, cols[h]], k[:, cols[h]], v[:, cols[h]], g[:, cols[h]]
        scores = (dot(qh, kh, NT) * decay).astype(BF16)
        grad_scores = (dot(gh, vh, NT) * decay).astype(BF16)
        out[:, cols[h]] = dot(scores, vh, NN)
        dq[:, cols[h]] = dot(grad_scores, kh, NN)
        dk[:, cols[h]] = dot(grad_scores, qh, TN)
        dv[:, cols[h]] = dot(scores, gh, TN)

    def in_blocks():
        for h in range(NH):
            within(h)
        given[...] = q[:, halves[0]].astype(F32)

    def wait_for(some):
        for fetch in some:
            fetch.wait()

    def local_states(way, heads, head_rates):
        for h, rate in zip(heads, head_rates):
            local_state(way, h, rate)

    last_out = (s == 0) & (x == 0)

    @pl.when(last_out)
    def _():
        wait_for(fetches[2:4])
        local_states(0, theirs, their_rates)

    @pl.when(jnp.logical_not(last_out))
    def _():
        wait_for(fetches[2:])
        for way in (0, 1):
            local_states(way, theirs, their_rates)
            local_states(way, mine, own_rates)
        in_blocks()

    pl.semaphore_wait(barrier, len(others) + jnp.minimum(z, 2) + jnp.minimum(zs - 1 - z, 2))

    meta_copy = copy(mymeta, pmeta, m_send.at[0], m_recv.at[0], partner)
    meta_copy.start()
    sends = [meta_copy]

    first_copies = [
        [
            copy(local.at[way, theirs[i]], part.at[way, i], d_send.at[way, i], d_recv.at[way, i], partner)
            for i in range(OWN)
        ]
        for way in (0, 1)
    ]
    sends.extend(first_copies[0] + first_copies[1])
    for first_copy in first_copies[0]:
        first_copy.start()

    @pl.when(last_out)
    def _():
        wait_for(fetches[4:6])
        local_states(0, mine, own_rates)

    @pl.when(jnp.logical_not(last_out))
    def _():
        for first_copy in first_copies[1]:
            first_copy.start()


    meta_copy.wait_recv()
    firsts = [jnp.where(c == 0, mymeta[0:1, :], pmeta[0:1, :]), jnp.where(c == 0, pmeta[0:1, :], mymeta[0:1, :])]
    lasts = [jnp.where(c == 0, mymeta[1:2, :], pmeta[1:2, :]), jnp.where(c == 0, pmeta[1:2, :], mymeta[1:2, :])]
    chip_meta = jnp.where(row_id == 0, jnp.broadcast_to(firsts[0], (8, DH)), jnp.broadcast_to(lasts[1], (8, DH)))
    cmeta[...] = chip_meta
    rmeta[y] = chip_meta
    same_chip = [(lasts[0] == lasts[1]).astype(F32), (firsts[0] == firsts[1]).astype(F32)]

    def row_send(way, i, n, j):
        rows = pl.ds(pl.multiple_of(j * width, width), width)
        return copy(
            chip.at[way, i, rows], there.at[way, i, y], t_send.at[way, i, n], t_recv.at[way, i, y], at(z, j, c)
        )

    def meta_send(n, j):
        return copy(cmeta, rmeta.at[y], m_send.at[1 + n], m_recv.at[1 + y], at(z, j, c))

    def back_send(way, i, n, j):
        rows = pl.ds(pl.multiple_of(y * width, width), width)
        return copy(
            slices.at[way, i, j], raw.at[way, i, rows], b_send.at[way, i, n], b_recv.at[way, i, y], at(z, j, c)
        )

    def core_send(way, i):
        return copy(give.at[way, i], state.at[way, mine[i]], e_send.at[way, i], e_recv.at[way, i], partner)

    def to_row(way):
        for i in range(OWN):
            first_copies[way][i].wait_recv()
            carried = jnp.exp(-own_rates[i] * BLK) * same_chip[way]
            mine = jnp.where(c == 1 - way, 1.0, carried)
            theirs = jnp.where(c == 1 - way, carried, 1.0)
            whole = mine * local[way, OWN * c + i] + theirs * part[way, i]
            chip[way, i] = whole
            for n, j in enumerate(in_row):
                row_send(way, i, n, j).start()
            there[way, i, y] = chip[way, i, pl.ds(pl.multiple_of(y * width, width), width), :]

    def send_meta():
        for n, j in enumerate(in_row):
            meta_send(n, j).start()

    @pl.when(z == 0)
    def _():
        to_row(0)
        send_meta()

        @pl.when(last_out)
        def _():
            wait_for(fetches[6:])
            local_states(1, theirs, their_rates)
            for first_copy in first_copies[1]:
                first_copy.start()
            local_states(1, mine, own_rates)

        to_row(1)

        @pl.when(last_out)
        def _():
            in_blocks()

    @pl.when(z != 0)
    def _():
        to_row(1)
        send_meta()
        to_row(0)

    gifts = [
        copy(given, got.at[0], g_send.at[0], g_recv.at[0], partner),
        copy(out.at[:, halves[0]], got.at[1], g_send.at[1], g_recv.at[1], partner),
    ]
    for gift in gifts:
        gift.start()
    sends.extend(gifts)

    for j in in_row:
        copy(cmeta, rmeta.at[j], m_send.at[0], m_recv.at[1 + j], partner).wait_recv()

    def end_of(way, j):
        return rmeta[j, 1:2, :] if way == 0 else rmeta[j, 0:1, :]

    def z_copy(way, n, i):
        rows = slice(0, 8 + width) if i == 0 else slice(8 + width, 8 + 2 * width)
        return copy(
            zsend.at[way, rows], zrecv.at[way, n - 1, rows], z_send.at[way, n - 1, i], z_recv.at[way, n - 1, i], hop(way, n)
        )

    orders = [list(range(ROW)), list(range(ROW))[::-1]]

    def row_copy(way, i, j):
        return copy(there.at[way, i, y], there.at[way, i, j], t_send.at[way, i, 0], t_recv.at[way, i, j], partner)

    def end_wait(way, i):
        end = orders[way][-1]

        @pl.when(y != end)
        def _():
            row_copy(way, i, end).wait_recv()

    def to_rows(way):
        order = orders[way]
        zsend[way, 0:8] = jnp.broadcast_to(end_of(way, order[-1]), (8, DH))
        for i in range(OWN):
            for j in in_row:

                @pl.when(j != order[-1])
                def _():
                    row_copy(way, i, j).wait_recv()

            span = jnp.exp(-own_rates[i] * (2 * BLK))
            sofar = there[way, i, order[0]]
            for n in range(1, ROW):
                slices[way, i, order[n]] = sofar
                keep = span * (end_of(way, order[n]) == end_of(way, order[n - 1])).astype(F32)
                if n < ROW - 1:
                    sofar = there[way, i, order[n]] + keep * sofar

            @pl.when(after(way) >= 1)
            def _():
                end_wait(way, i)
                zsend[way, 8 + i * width : 8 + (i + 1) * width] = there[way, i, order[-1]] + keep * sofar
                z_copy(way, 1, i).start()

            @pl.when(after(way) >= 2)
            def _():
                z_copy(way, 2, i).start()


    def to_chips(way):
        order = orders[way]
        for i in range(OWN):
            for n in (1, 2):

                @pl.when(before(way) >= n)
                def _():
                    z_copy(way, n, i).wait_recv()

            if i == 0:
                near, far = zrecv[way, 0, 0:1], zrecv[way, 1, 0:1]
            span = jnp.exp(-own_rates[i] * (2 * BLK))
            row_span = jnp.exp(-own_rates[i] * (2 * BLK * ROW)) * (near == far).astype(F32)
            rows = slice(8 + i * width, 8 + (i + 1) * width)
            entering = zrecv[way, 0, rows] + row_span * zrecv[way, 1, rows]
            keep = jnp.ones((1, DH), F32)
            there_end = near
            for n in range(ROW):
                j = order[n]
                if n == 0:
                    slices[way, i, j] = entering
                else:
                    slices[way, i, j] = slices[way, i, j] + keep * entering
                here = end_of(way, j)
                keep = keep * span * (here == there_end).astype(F32)
                there_end = here
            for n, j in enumerate(in_row):
                back_send(way, i, n, j).start()
            here = pl.ds(pl.multiple_of(y * width, width), width)
            raw[way, i, here] = slices[way, i, y]

    @pl.when(z == 0)
    def _():
        for way in (0, 1):
            to_rows(way)
            to_chips(way)

    @pl.when(z != 0)
    def _():
        to_rows(1)
        to_rows(0)
        to_chips(0)
        to_chips(1)

    beside = []
    for way in (0, 1):
        neighbour = rmeta[(y + ROW - 1) % ROW, 1:2, :] if way == 0 else rmeta[(y + 1) % ROW, 0:1, :]
        beside.append(jnp.where(y == (0 if way == 0 else ROW - 1), zrecv[way, 0, 0:1], neighbour))

    def to_core(way):
        inner = lasts[0] if way == 0 else firsts[1]
        kept = (inner == beside[way]).astype(F32)
        for i in range(OWN):
            for j in in_row:
                there_rows = pl.ds(pl.multiple_of(j * width, width), width)
                copy(
                    slices.at[way, i, j], raw.at[way, i, there_rows], b_send.at[way, i, 0], b_recv.at[way, i, j], partner
                ).wait_recv()
            outer = raw[way, i]
            between = jnp.where(c == way, local[way, OWN * c + i], part[way, i])
            inside = between + jnp.exp(-own_rates[i] * BLK) * kept * outer
            give[way, i] = jnp.where(c == way, inside, outer)
            core_send(way, i).start()
            state[way, OWN * c + i] = jnp.where(c == way, outer, inside)

    def from_core(way):
        for i in range(OWN):
            copy(
                give.at[way, i], state.at[way, OWN * (1 - c) + i], e_send.at[way, i], e_recv.at[way, i], partner
            ).wait_recv()

    seg_before = jnp.where(c == 0, beside[0], lasts[0])
    seg_after = jnp.where(c == 1, beside[1], firsts[1])
    joins = (seg_cols == seg_before).astype(F32)
    leaves = (seg_cols == seg_after).astype(F32)
    partner_cols = jnp.broadcast_to(pmeta[2:3, :], (BLK, BLK)).T
    partner_joins = (partner_cols == jnp.where(c == 1, beside[0], lasts[0])).astype(F32)
    for i in range(OWN):
        weight = jnp.exp(-own_rates[i] * (place + 1.0))
        inw[0, i] = weight * joins
        inw[1, i] = weight * partner_joins
        inw[2, i] = jnp.exp(-their_rates[i] * (place + 1.0)) * joins
        outw[0, i] = jnp.exp(-own_rates[i] * (BLK - place)) * leaves
        outw[1, i] = jnp.exp(-their_rates[i] * (BLK - place)) * leaves
    for gift in gifts:
        gift.wait_recv()
    for n, j in enumerate(in_row):
        meta_send(n, j).wait_send()
    for way in (0, 1):
        for i in range(OWN):
            for n, j in enumerate(in_row):
                row_send(way, i, n, j).wait_send()
    for sent in sends:
        sent.wait_send()
    for w, n in hops:
        for i in range(OWN):

            @pl.when(after(w) >= n)
            def _():
                z_copy(w, n, i).wait_send()

    to_core(0)

    def output(within_out, query, entering, weight):
        high, low = split(entering)
        return within_out + weight * (dot(query, high, NN) + dot(query, low, NN))

    squares, partner_squares = jnp.zeros((BLK, DH), F32), jnp.zeros((BLK, DH), F32)
    for i in range(OWN):
        whole = output(got[1, :, cols[i]], got[0, :, cols[i]].astype(BF16), give[0, i], inw[1, i])
        pout[:, cols[i]] = whole
        partner_squares = partner_squares + whole * whole
        at_mine = columns(mine[i])
        whole = output(out[:, at_mine], q[:, at_mine], state[0, mine[i]], inw[0, i])
        out[:, at_mine] = whole
        squares = squares + whole * whole

    def row_of(total):
        return jnp.broadcast_to(jnp.sum(total.T, axis=0, keepdims=True), (8, DH))

    xsend[0] = row_of(squares)
    xsend[1] = row_of(partner_squares)
    last_sends = [
        copy(xsend.at[m], xrecv.at[c, x], x_send.at[m, n], x_recv.at[c, x], (to, (x + n) % xs))
        for n in x_first
        for m, to in ((0, s), (1, partner[0]))
    ]
    last_sends.append(copy(xsend.at[1], xrecv.at[c, x], x_send.at[1, 0], x_recv.at[c, x], partner))
    for sent in last_sends:
        sent.start()
    out_copy = copy(pout, outgot, o_send.at[0], o_recv.at[0], partner)
    out_copy.start()
    xrecv[c, x] = xsend[0]

    to_core(1)

    def grad_query(h, inflow):
        high, low = split(state[0, h])
        gh = g[:, columns(h)]
        dq[:, columns(h)] = dq[:, columns(h)] + inflow * (dot(gh, high, NT) + dot(gh, low, NT))

    def grad_key_value(h, outflow):
        high, low = split(state[1, h])
        kh, vh = k[:, columns(h)], v[:, columns(h)]
        dk[:, columns(h)] = dk[:, columns(h)] + outflow * (dot(vh, high, NT) + dot(vh, low, NT))
        dv[:, columns(h)] = dv[:, columns(h)] + outflow * (dot(kh, high, NN) + dot(kh, low, NN))

    for i in range(OWN):
        grad_key_value(mine[i], outw[0, i])
        grad_query(mine[i], inw[0, i])
    from_core(0)
    for i in range(OWN):
        grad_query(theirs[i], inw[2, i])
    from_core(1)
    for i in range(OWN):
        grad_key_value(theirs[i], outw[1, i])

    for way in (0, 1):

        @pl.when(after(way) < 1)
        def _():
            for i in range(OWN):
                end_wait(way, i)

    out_copy.wait_recv()
    for way in (0, 1):
        for i in range(OWN):
            for n, j in enumerate(in_row):
                back_send(way, i, n, j).wait_send()
            core_send(way, i).wait_send()
    out_copy.wait_send()
    for m in (c, 1 - c):
        for n in (x_first if m is c else [*x_first, 0]):
            from_x = (x + n) % xs
            copy(xsend.at[0], xrecv.at[m, from_x], x_send.at[0, n], x_recv.at[m, from_x], partner).wait_recv()
    summed = xrecv[0, 0] + xrecv[1, 0]
    for n in range(1, xs):
        summed = summed + (xrecv[0, n] + xrecv[1, n])
    inverse = lax.rsqrt(summed / (NH * DH * xs) + EPSILON)
    scale = jnp.broadcast_to(inverse[0:1, :], (BLK, BLK)).T
    for i in range(OWN):
        at_mine, at_theirs = columns(mine[i]), columns(theirs[i])
        normed[:, at_mine] = out[:, at_mine] * gain[:, at_mine] * scale
        normed[:, at_theirs] = outgot[:, cols[i]] * gain[:, at_theirs] * scale
    for sent in last_sends:
        sent.wait_send()


def finish(*refs):
    sems = refs[8]
    rows = [pl.ds(n * BLK // PIECES, BLK // PIECES) for n in range(PIECES)]
    stores = [
        pltpu.make_async_copy(refs[n].at[piece], refs[4 + n].at[piece], sems.at[n, m])
        for n in range(4)
        for m, piece in enumerate(rows)
    ]
    for store in stores:
        store.start()
    for store in stores:
        store.wait()


def body(zs, xs, queries, keys, values, d_out, segment_ids, decay_exps, gain):
    width = BLK // ROW
    vmem = pl.BlockSpec(memory_space=pltpu.VMEM)
    dma = pltpu.SemaphoreType.DMA
    result = jax.ShapeDtypeStruct((BLK, NH * DH), F32)
    operands = (
        decay_exps, segment_ids.reshape(1, BLK), queries, keys, values, d_out, gain.reshape(1, NH * DH)
    )
    held = pl.pallas_call(
        functools.partial(kernel, zs, xs),
        out_shape=(result,) * 4,
        in_specs=[pl.BlockSpec(memory_space=pltpu.HBM)] * 7,
        out_specs=(vmem,) * 4,
        scratch_shapes=[
            pltpu.SMEM((NH,), jnp.int32),
            pltpu.VMEM((1, BLK), jnp.int32),
            *[pltpu.VMEM((BLK, NH * DH), BF16)] * 4,
            pltpu.VMEM((1, NH * DH), F32),
            pltpu.VMEM((2, NH, DH, DH), F32),
            pltpu.VMEM((2, OWN, DH, DH), F32),
            pltpu.VMEM((8, DH), F32),
            pltpu.VMEM((8, DH), F32),
            pltpu.VMEM((2, OWN, DH, DH), F32),
            pltpu.VMEM((8, DH), F32),
            pltpu.VMEM((ROW, 8, DH), F32),
            pltpu.VMEM((2, OWN, ROW, width, DH), F32),
            pltpu.VMEM((2, 8 + OWN * width, DH), F32),
            pltpu.VMEM((2, 2, 8 + OWN * width, DH), F32),
            pltpu.VMEM((2, OWN, ROW, width, DH), F32),
            pltpu.VMEM((2, OWN, DH, DH), F32),
            pltpu.VMEM((2, OWN, DH, DH), F32),
            pltpu.VMEM((2, NH, DH, DH), F32),
            pltpu.VMEM((BLK, NH * DH), F32),
            pltpu.VMEM((3, OWN, BLK, DH), F32),
            pltpu.VMEM((2, OWN, BLK, DH), F32),
            pltpu.VMEM((BLK, OWN * DH), F32),
            pltpu.VMEM((2, BLK, OWN * DH), F32),
            pltpu.VMEM((BLK, OWN * DH), F32),
            pltpu.VMEM((BLK, OWN * DH), F32),
            pltpu.VMEM((2, 8, DH), F32),
            pltpu.VMEM((2, xs, 8, DH), F32),
            dma((9,)),
            dma((2,)), dma((2,)),
            dma((1,)), dma((1,)),
            dma((2, OWN)), dma((2, OWN)),
            dma((1 + ROW,)), dma((1 + ROW,)),
            dma((2, OWN, ROW)), dma((2, OWN, ROW)),
            dma((2, 2, OWN)), dma((2, 2, OWN)),
            dma((2, OWN, ROW)), dma((2, OWN, ROW)),
            dma((2, OWN)), dma((2, OWN)),
            dma((2, xs)), dma((2, xs)),
        ],
        compiler_params=pltpu.CompilerParams(
            collective_id=0, has_side_effects=True, vmem_limit_bytes=32 << 20
        ),
        name="attention",
    )(*(pltpu.with_memory_space_constraint(operand, pltpu.HBM) for operand in operands))
    return pl.pallas_call(
        finish,
        out_shape=(result,) * 4,
        in_specs=[vmem] * 4,
        out_specs=(pl.BlockSpec(memory_space=pl.ANY),) * 4,
        scratch_shapes=[dma((4, PIECES))],
        name="finish",
    )(*(pltpu.with_memory_space_constraint(part, pltpu.VMEM) for part in held))


def solution(mesh):
    both = P("seq", "head")
    return jax.shard_map(
        functools.partial(body, mesh.shape["seq"] // (2 * ROW), mesh.shape["head"]),
        mesh=mesh,
        in_specs=(both, both, both, both, P("seq"), P("head"), P("head")),
        out_specs=(both, both, both, both),
        check_vma=False,
    )
```
